128 devices in a mesh: section: 8 (over z, y_lo), fsdp: 16 (over y_hi, x, core).
Axes of the slice: x: 4, y: 4 (y_hi: 2, y_lo: 2; y = y_hi * 2 + y_lo), z: 4, core: 2. Of those that a mesh axis runs over, the one named last changes fastest.
Arguments:
- activations: bfloat16 [8, 512, 5120], P('section', 'fsdp'), may hold values from -0.625 to 0.625
- gate_preact: bfloat16 [8, 512, 14336], P('section', None, 'fsdp'), may hold values from -6 to 6
- hidden_grad: bfloat16 [8, 512, 14336], P('section', None, 'fsdp'), may hold values from -6 to 6
- up_weight: bfloat16 [8, 5120, 14336], P('section', None, 'fsdp'), may hold values from -0.046875 to 0.046875
- resid_grad: bfloat16 [8, 512, 5120], P('section', 'fsdp'), may hold values from -6 to 6
- feedback: float32 [8, 512, 5120], P('section', 'fsdp'), may hold values from -4 to 4
- start_basis: float32 [8, 5120, 64], P('section'), may hold values from -6 to 6
Outputs:
- up_grad: bfloat16 [8, 5120, 14336], P('section', None, 'fsdp')
- new_feedback: float32 [8, 512, 5120], P('section', 'fsdp')
- received: float32 [8, 512, 5120], P('section', 'fsdp')
The draws below stay inside these ranges and needn't reach their ends.
All inputs are finite; a program needn't handle non-finite values.
Results may differ from the reference program's by a relative error of at most 0.005.
Values may be sent and summed in bfloat16 or wider, within the bound.
No kernel may reach another device: no remote copies, remote signals or barrier semaphores. Data moves between devices by JAX's collectives and lax.ppermute only.
A program may use at most 128 MiB of HBM per device.

```python
import jax
import jax.numpy as jnp
from jax import lax

D = 5120
FF = 14336
RANK = 64
TOKENS = 512
N_SECTION = 8


def strengthened(array, own_key, source, target, parts, factor):
    owner, partner = [(jnp.arange(array.shape[axis_at]) // (array.shape[axis_at] // parts)).reshape([-1 if axis == axis_at else 1 for axis in range(array.ndim)]) for axis_at in (source, target)]
    chosen = jax.random.permutation(own_key, parts)[partner]
    strong = (owner == chosen) | (owner == (partner + parts // 2) % parts)
    return jnp.where(strong, factor * array, array)


def block_scale(rng, dims, shards, smallest, top_value):
    gain = 1.0
    for position, blocks in shards:
        draws = jax.random.uniform(jax.random.fold_in(jax.random.fold_in(rng, 6), position), (blocks,), jnp.float32, smallest / len(shards), top_value / len(shards))
        gain = gain * jnp.repeat(jnp.exp(draws), dims[position] // blocks).reshape((-1,) + (1,) * (len(dims) - 1 - position))
    return gain


def normal_values(stream_key, shape, spread, bound, pieces=(), dtype=jnp.bfloat16):
    loudness = block_scale(stream_key, shape, pieces, -0.22, 0.18) if pieces else 1.0
    entries = jax.random.normal(stream_key, shape, jnp.float32) * spread * loudness
    return jnp.minimum(jnp.maximum(entries, -bound), bound).astype(dtype)


def noise_with(rng, shape, width, reach, shards, heavy, kind=jnp.bfloat16):
    array = width * jax.random.normal(rng, shape, jnp.float32)
    if shards:
        array = array * block_scale(rng, shape, shards, -0.22, 0.18)
    return jnp.clip(strengthened(array, jax.random.fold_in(rng, 3), *heavy), -reach, reach).astype(kind)


def setup_inputs(seed: int = 0) -> dict:
    seeds = jax.random.split(jax.random.key(seed), 8)
    return {
        "activations": normal_values(seeds[0], (N_SECTION, TOKENS, D), (TOKENS ** -0.5), 0.625, ((0, 8), (1, 16))),
        "gate_preact": normal_values(seeds[1], (N_SECTION, TOKENS, FF), 1.0, 6.0, ((0, 8), (2, 16))),
        "hidden_grad": noise_with(seeds[2], (N_SECTION, TOKENS, FF), 1.0, 6.0, ((0, 8), (2, 16)), (2, 1, 16, 2.0)),
        "up_weight": normal_values(seeds[3], (N_SECTION, D, FF), FF ** -0.5, 0.046875, ((0, 8), (2, 16))),
        "resid_grad": normal_values(seeds[4], (N_SECTION, TOKENS, D), 0.5, 6.0, ((0, 8), (1, 16))),
        "feedback": normal_values(seeds[5], (N_SECTION, TOKENS, D), 0.3, 4.0, ((0, 8), (1, 16)), jnp.float32),
        "start_basis": normal_values(seeds[6], (N_SECTION, D, RANK), 1.0, 6.0, ((0, 8),), jnp.float32),
    }


def section_math(activations, gate_preact, hidden_grad, up_weight, resid_grad, feedback, start_basis):
    highest = lax.Precision.HIGHEST
    unit_grad = (hidden_grad.astype(jnp.float32) * jax.nn.silu(gate_preact.astype(jnp.float32))).astype(jnp.bfloat16)
    up_grad = jnp.dot(activations.T.astype(jnp.float32), unit_grad.astype(jnp.float32), preferred_element_type=jnp.float32).astype(jnp.bfloat16)
    input_grad = jnp.dot(unit_grad.astype(jnp.float32), up_weight.T.astype(jnp.float32), preferred_element_type=jnp.float32)
    merged = resid_grad.astype(jnp.float32) + feedback + input_grad
    raw_left = jnp.dot(merged, start_basis, precision=highest)
    gram_total = jnp.dot(raw_left.T, raw_left, precision=highest)
    lower_factor = jnp.linalg.cholesky(gram_total)
    left_factor = lax.linalg.triangular_solve(lower_factor, raw_left, left_side=False, lower=True, transpose_a=True)
    right_factor = jnp.dot(merged.T, left_factor, precision=highest)
    approximation = jnp.dot(left_factor, right_factor.T, precision=highest)
    new_feedback = merged - approximation
    return (up_grad, new_feedback, approximation)

def reference(activations, gate_preact, hidden_grad, up_weight, resid_grad, feedback, start_basis):
    grads = []
    feedbacks = []
    rebuilt = []
    for section_index in range(N_SECTION):
        outputs = section_math(activations[section_index], gate_preact[section_index], hidden_grad[section_index], up_weight[section_index], resid_grad[section_index], feedback[section_index], start_basis[section_index])
        grads.append(outputs[0])
        feedbacks.append(outputs[1])
        rebuilt.append(outputs[2])
    shifted = rebuilt[1:] + [jnp.zeros((TOKENS, D), jnp.float32)]
    return (jnp.stack(grads), jnp.stack(feedbacks), jnp.stack(shifted))
```

```python
import jax
import jax.numpy as jnp
from jax import lax
from jax.experimental import pallas as pl
from jax.experimental.pallas import tpu as pltpu
from jax.sharding import PartitionSpec as P

D = 5120
F = 896
R = 64
T = 512
TILE = 640
STEPS = D // TILE
BF = jnp.bfloat16
F32 = jnp.float32
VMEM_LIMIT = 50 * 1024 * 1024


def params():
    return pltpu.CompilerParams(vmem_limit_bytes=VMEM_LIMIT)


def place():
    index = lax.axis_index("fsdp")
    y, x, core = index // 8, (index // 2) % 4, index % 2
    return index, y, x, core


def xor_x(x, mask):
    return x + mask - 2 * (x & mask)


def pieces(value, count):
    out = []
    for _ in range(count):
        part = value.astype(BF)
        out.append(part)
        value = value - part.astype(F32)
    return out


def nn(a, b):
    return lax.dot_general(a, b, (((1,), (0,)), ((), ())), preferred_element_type=F32)


def nt(a, b):
    return lax.dot_general(a, b, (((1,), (1,)), ((), ())), preferred_element_type=F32)


def tn(a, b):
    return lax.dot_general(a, b, (((0,), (0,)), ((), ())), preferred_element_type=F32)


def row_blocks(y, x, core):
    out = []
    for c in (1 - core, core):
        first, second = 1 + 2 * c, 3 - 2 * c
        for xx in (xor_x(x, 2), xor_x(x, first), xor_x(x, second), x):
            for yy in (1 - y, y):
                out.append(yy * 8 + xx * 2 + c)
    return out


def unit_kernel(gate, hidden, weight, basis, resid, feedback, unit, ordered, raw_t, wb, rb):
    step = pl.program_id(0)

    @pl.when(step == 0)
    def _():
        wb[...] = jnp.zeros_like(wb)
        rb[...] = jnp.zeros_like(rb)

    split = jnp.concatenate(pieces(basis[...], 3), axis=1)
    wb[...] += tn(split, weight[...])
    rows = jnp.concatenate(pieces(resid[...].astype(F32) + feedback[...], 3), axis=0)
    rb[...] += tn(split, rows.T)
    g = gate[...].astype(F32)
    unit[pl.ds(step * 64, 64), :] = (hidden[...].astype(F32) * (g / (1.0 + jnp.exp(-g)))).astype(BF)

    @pl.when(step == STEPS - 1)
    def _():
        index, y, x, core = place()
        for place_to, block in enumerate(row_blocks(y, x, core)):
            ordered[pl.ds(place_to * 32, 32), :] = unit[pl.ds(pl.multiple_of(block * 32, 32), 32), :]
        total = wb[0:R, :] + wb[R : 2 * R, :] + wb[2 * R : 3 * R, :]
        raw3 = nt(jnp.concatenate(pieces(total, 3), axis=0), unit[...])
        raw = raw3[0:R] + raw3[R : 2 * R] + raw3[2 * R : 3 * R]
        own = rb[0:R] + rb[R : 2 * R] + rb[2 * R : 3 * R]
        own = own[:, 0:32] + own[:, 32:64] + own[:, 64:96]
        spot = lax.broadcasted_iota(jnp.int32, (32, T), 1) - index * 32
        select = (spot == lax.broadcasted_iota(jnp.int32, (32, T), 0)).astype(BF)
        placed = nn(jnp.concatenate(pieces(own, 3), axis=0), select)
        raw_t[...] = raw + placed[0:R] + placed[R : 2 * R] + placed[2 * R : 3 * R]


def unit_call(gate, hidden, weight, basis, resid, feedback):
    return pl.pallas_call(
        unit_kernel,
        grid=(STEPS,),
        in_specs=[
            pl.BlockSpec((64, F), lambda i: (i, 0)),
            pl.BlockSpec((64, F), lambda i: (i, 0)),
            pl.BlockSpec((TILE, F), lambda i: (i, 0)),
            pl.BlockSpec((TILE, R), lambda i: (i, 0)),
            pl.BlockSpec((32, TILE), lambda i: (0, i)),
            pl.BlockSpec((32, TILE), lambda i: (0, i)),
        ],
        out_specs=[
            pl.BlockSpec((T, F), lambda i: (0, 0)),
            pl.BlockSpec((T, F), lambda i: (0, 0)),
            pl.BlockSpec((R, T), lambda i: (0, 0)),
        ],
        out_shape=[
            jax.ShapeDtypeStruct((T, F), BF),
            jax.ShapeDtypeStruct((T, F), BF),
            jax.ShapeDtypeStruct((R, T), F32),
        ],
        scratch_shapes=[pltpu.VMEM((3 * R, F), F32), pltpu.VMEM((3 * R, 96), F32)],
        compiler_params=params(),
        cost_estimate=pl.CostEstimate(flops=2 * D * F * 192, bytes_accessed=15_000_000, transcendentals=T * F),
        name="unit_and_raw",
    )(gate, hidden, weight, basis, resid, feedback)


def partial_kernel(unit, weight, first, second):
    product = nt(unit[...], weight[...])
    first[...] = product[0:128].astype(first.dtype)
    second[...] = product[128:256].astype(second.dtype)


def partial_call(ordered, half, weight, dtype, name):
    return pl.pallas_call(
        partial_kernel,
        grid=(STEPS,),
        in_specs=[
            pl.BlockSpec((256, F), lambda i: (half, 0)),
            pl.BlockSpec((TILE, F), lambda i: (i, 0)),
        ],
        out_specs=[pl.BlockSpec((128, TILE), lambda i: (0, i))] * 2,
        out_shape=[jax.ShapeDtypeStruct((128, D), dtype)] * 2,
        compiler_params=params(),
        cost_estimate=pl.CostEstimate(flops=2 * 256 * F * D, bytes_accessed=13_000_000, transcendentals=0),
        name=name,
    )(ordered, weight)


def eliminated(gram):
    rows = lax.broadcasted_iota(jnp.int32, (R, 2 * R), 0)
    lanes = lax.broadcasted_iota(jnp.int32, (R, 2 * R), 1)
    work = jnp.concatenate([gram, jnp.zeros((R, R), F32)], axis=1)
    work = jnp.where(lanes == rows + R, 1.0, work)
    scales = []
    for j in range(R):
        column = work[:, j : j + 1]
        pivot = column[j : j + 1, :]
        row = work[j : j + 1, :]
        scales.append(row * lax.rsqrt(pivot))
        work = work - jnp.where(rows[:, 0:1] > j, column, 0.0) * (row / pivot)
    return jnp.concatenate(scales, axis=0)[:, R:]


def exact(op, a, b):
    a1, a2, a3 = pieces(a, 3)
    b1, b2, b3 = pieces(b, 3)
    low = op(a1, b3) + op(a2, b2) + op(a3, b1)
    return op(a1, b1) + (op(a1, b2) + op(a2, b1) + low)


def factor_kernel(raw_a, raw_b, unit, weight, resid, feedback, own_out, other_out, left, z, left_t):
    step = pl.program_id(0)
    index, y, x, core = place()

    @pl.when(step == 0)
    def _():
        raw = raw_a[...] + raw_b[...]
        gram = exact(nt, raw, raw)
        inverse = eliminated(gram)
        basis = exact(nn, inverse, raw)
        parts = jnp.concatenate(pieces(basis, 3), axis=0)
        z3 = nn(parts, unit[...])
        z[...] = jnp.concatenate(pieces(z3[0:R] + z3[R : 2 * R] + z3[2 * R : 3 * R], 2), axis=0)
        spot = lax.broadcasted_iota(jnp.int32, (32, T), 1) - index * 32
        select = (spot == lax.broadcasted_iota(jnp.int32, (32, T), 0)).astype(BF)
        own3 = nt(select, parts)
        left[...] = own3[:, 0:R] + own3[:, R : 2 * R] + own3[:, 2 * R : 3 * R]
        own_t = nt(parts, select)
        left_t[...] = own_t[0:R] + own_t[R : 2 * R] + own_t[2 * R : 3 * R]

    both = nt(z[...], weight[...])
    value = both[0:R] + both[R : 2 * R]
    l1, l2 = pieces(left_t[...], 2)
    r1, r2 = pieces(resid[...].astype(F32) + feedback[...], 2)
    value = value + (nn(l1, r1) + (nn(l1, r2) + nn(l2, r1)))
    half = step // 4
    chunk = step % 4
    for c in (0, 1):
        first = 1 + 2 * c
        apart = xor_x(chunk, x)
        spot = jnp.where(apart == 0, 3, jnp.where(apart == 2, 0, jnp.where(apart == first, 1, 2)))

        @pl.when((half == c) & (core == c))
        def _():
            own_out[spot] = value

        @pl.when((half == c) & (core != c))
        def _():
            other_out[spot] = value.astype(BF)


def factor_call(raw_a, raw_b, unit, weight, resid, feedback):
    return pl.pallas_call(
        factor_kernel,
        grid=(STEPS,),
        in_specs=[
            pl.BlockSpec((R, T), lambda i: (0, 0)),
            pl.BlockSpec((R, T), lambda i: (0, 0)),
            pl.BlockSpec((T, F), lambda i: (0, 0)),
            pl.BlockSpec((TILE, F), lambda i: (i, 0)),
            pl.BlockSpec((32, TILE), lambda i: (0, i)),
            pl.BlockSpec((32, TILE), lambda i: (0, i)),
        ],
        out_specs=[
            pl.BlockSpec((4, R, TILE), lambda i: (0, 0, 0)),
            pl.BlockSpec((4, R, TILE), lambda i: (0, 0, 0)),
            pl.BlockSpec((32, R), lambda i: (0, 0)),
        ],
        out_shape=[
            jax.ShapeDtypeStruct((4, R, TILE), F32),
            jax.ShapeDtypeStruct((4, R, TILE), BF),
            jax.ShapeDtypeStruct((32, R), F32),
        ],
        scratch_shapes=[pltpu.VMEM((2 * R, F), BF), pltpu.VMEM((R, 32), F32)],
        compiler_params=params(),
        cost_estimate=pl.CostEstimate(flops=2 * D * F * 192, bytes_accessed=12_000_000, transcendentals=0),
        name="factor",
    )(raw_a, raw_b, unit, weight, resid, feedback)


def grad_kernel(*refs):
    unit, out = refs[8], refs[9]
    tokens = jnp.concatenate([ref[...] for ref in refs[:8]], axis=0)
    out[...] = tn(tokens, unit[...]).astype(BF)


def grad_call(pairs, ordered):
    return pl.pallas_call(
        grad_kernel,
        grid=(STEPS,),
        in_specs=[pl.BlockSpec((64, TILE), lambda i: (0, i))] * 8 + [pl.BlockSpec((T, F), lambda i: (0, 0))],
        out_specs=pl.BlockSpec((TILE, F), lambda i: (i, 0)),
        out_shape=jax.ShapeDtypeStruct((D, F), BF),
        compiler_params=params(),
        cost_estimate=pl.CostEstimate(flops=2 * D * F * T, bytes_accessed=16_000_000, transcendentals=0),
        name="weight_grad",
    )(*pairs, ordered)


def final_kernel(*refs):
    chunks, (left, left_next, resid, feedback, mine, partner, out, received) = refs[:8], refs[8:]
    _, _, x, core = place()
    l3 = jnp.concatenate(pieces(left[...], 2), axis=0)
    n3 = jnp.concatenate(pieces(left_next[...], 2), axis=0)
    for h in (0, 1):
        c = core if h == 0 else 1 - core
        first, second = 1 + 2 * c, 3 - 2 * c
        for k, xx in enumerate((xor_x(x, 2), xor_x(x, first), xor_x(x, second), x)):
            columns = pl.ds(pl.multiple_of((c * 4 + xx) * TILE, 128), TILE)
            chunk = chunks[h * 4 + k]
            here = nn(l3, chunk[0])
            there = nn(n3, chunk[1])
            merged = resid[:, columns].astype(F32) + feedback[:, columns]
            merged = merged + (mine[:, columns] + partner[:, columns].astype(F32))
            out[:, columns] = merged - (here[0:32] + here[32:64])
            received[:, columns] = there[0:32] + there[32:64]


def final_call(chunks, left, left_next, resid, feedback, mine, partner):
    vmem = pl.BlockSpec(memory_space=pltpu.VMEM)
    return pl.pallas_call(
        final_kernel,
        in_specs=[vmem] * 14,
        out_specs=[vmem, vmem],
        out_shape=[jax.ShapeDtypeStruct((32, D), F32)] * 2,
        compiler_params=params(),
        cost_estimate=pl.CostEstimate(flops=2 * 4 * 32 * R * D, bytes_accessed=5_000_000, transcendentals=0),
        name="feedback_and_received",
    )(*chunks, left, left_next, resid, feedback, mine, partner)


def sent(value, move):
    pairs = []
    for index in range(16):
        y, x, core = move(index // 8, (index // 2) % 4, index % 2)
        pairs.append((index, y * 8 + x * 2 + core))
    return lax.ppermute(value, "fsdp", pairs)


def to_core(value):
    return sent(value, lambda y, x, c: (y, x, 1 - c))


def to_first(value):
    return sent(value, lambda y, x, c: (y, x ^ (1 + 2 * c), c))


def to_second(value):
    return sent(value, lambda y, x, c: (y, x ^ (3 - 2 * c), c))


def to_y(value):
    return sent(value, lambda y, x, c: (1 - y, x, c))


def to_previous(value):
    return lax.ppermute(value, "section", [(s, s - 1) for s in range(1, 8)])


def on_device(activations, gate_preact, hidden_grad, up_weight, resid_grad, feedback, start_basis):
    acts, weight, resid, fb = activations[0], up_weight[0], resid_grad[0], feedback[0]

    pair = jnp.concatenate([to_y(acts), acts], axis=0)
    unit, ordered, raw = unit_call(gate_preact[0], hidden_grad[0], weight, start_basis[0], resid, fb)
    pair_first = to_first(pair)
    pair_second, pair_both = to_second(pair), to_second(pair_first)
    own_pairs = [pair_both, pair_first, pair_second, pair]
    other_pairs = [to_core(value) for value in own_pairs]

    raw = raw + to_core(raw)
    raw = raw + to_first(raw)
    raw = raw + to_second(raw)
    raw_far = to_y(raw)

    other_a, other_b = partial_call(ordered, 0, weight, BF, "input_grad_other")
    own_a, own_b = partial_call(ordered, 1, weight, F32, "input_grad_own")
    come_a, come_b = to_core(other_a), to_core(other_b)
    come_first = to_first((own_a + come_a.astype(F32)).astype(BF))
    kept = own_b + come_b.astype(F32) + come_first.astype(F32)
    come_second = to_second(kept[0:64].astype(BF))
    kept = kept[64:128] + come_second.astype(F32)
    mine, partner = kept[32:64], to_y(kept[0:32].astype(BF))

    own, other, left = factor_call(raw, raw_far, unit, weight, resid, fb)
    left_next = to_previous(left)
    come = to_core(other)
    come_first = to_first((own[0:2] + come[0:2].astype(F32)).astype(BF))
    kept = own[2:4] + come[2:4].astype(F32) + come_first.astype(F32)
    come_second = to_second(kept[0].astype(BF))
    half_sum = (kept[1] + come_second.astype(F32)).astype(BF)
    right = (half_sum.astype(F32) + to_y(half_sum).astype(F32)).astype(BF)
    both = jnp.stack([right, to_previous(right)])
    both_first = to_first(both)
    both_second, both_far = to_second(both), to_second(both_first)
    own_chunks = [both_far, both_first, both_second, both]
    chunks = own_chunks + [to_core(value) for value in own_chunks]

    weight_grad = grad_call(other_pairs + own_pairs, ordered)
    new_feedback, received = final_call(chunks, left, left_next, resid, fb, mine, partner)
    return (weight_grad[None], new_feedback[None], received[None])


def solution(mesh):
    return jax.shard_map(
        on_device,
        mesh=mesh,
        in_specs=(
            P("section", "fsdp", None),
            P("section", None, "fsdp"),
            P("section", None, "fsdp"),
            P("section", None, "fsdp"),
            P("section", "fsdp", None),
            P("section", "fsdp", None),
            P("section", None, None),
        ),
        out_specs=(
            P("section", None, "fsdp"),
            P("section", "fsdp", None),
            P("section", "fsdp", None),
        ),
        check_vma=False,
    )
```

```python
import jax
import jax.numpy as jnp
from jax import lax
from jax.experimental import pallas as pl
from jax.experimental.pallas import tpu as pltpu
from jax.sharding import PartitionSpec as P

D = 5120
F = 896
R = 64
T = 512
TILE = 640
STEPS = D // TILE
BF = jnp.bfloat16
F32 = jnp.float32
VMEM_LIMIT = 24 * 1024 * 1024


def params(limit=VMEM_LIMIT):
    return pltpu.CompilerParams(vmem_limit_bytes=limit)


def place():
    index = lax.axis_index("fsdp")
    y, x, core = index // 8, (index // 2) % 4, index % 2
    return index, y, x, core


def xor_x(x, mask):
    return x + mask - 2 * (x & mask)


def pieces(value, count):
    out = []
    for _ in range(count):
        part = value.astype(BF)
        out.append(part)
        value = value - part.astype(F32)
    return out


def nn(a, b):
    return lax.dot_general(a, b, (((1,), (0,)), ((), ())), preferred_element_type=F32)


def nt(a, b):
    return lax.dot_general(a, b, (((1,), (1,)), ((), ())), preferred_element_type=F32)


def tn(a, b):
    return lax.dot_general(a, b, (((0,), (0,)), ((), ())), preferred_element_type=F32)


def row_blocks(y, x, core):
    out = []
    for c in (1 - core, core):
        first, second = 1 + 2 * c, 3 - 2 * c
        for xx in (xor_x(x, 2), xor_x(x, first), xor_x(x, second), x):
            for yy in (1 - y, y):
                out.append(yy * 8 + xx * 2 + c)
    return out


def unit_kernel(
    gate_hbm, hidden_hbm, weight, basis_hbm, resid_hbm, fb_hbm,
    unit, ordered, raw_t, held, gate, hidden, basis_t, resid, feedback, small, sems,
):
    def copied(source, target, sem):
        copy = pltpu.make_async_copy(source, target, sem)
        copy.start()
        return copy

    loads = []
    for k, (source, target) in enumerate(((basis_hbm, basis_t), (resid_hbm, resid), (fb_hbm, feedback))):
        loads.append(copied(source, target, small.at[k]))
    copies = []
    for i in range(STEPS):
        rows = pl.ds(i * TILE, TILE)
        copies.append(copied(weight.at[rows], held.at[rows], sems.at[i]))
        if i == 1:
            loads.append(copied(gate_hbm, gate, small.at[3]))
            loads.append(copied(hidden_hbm, hidden, small.at[4]))
    for load in loads[:3]:
        load.wait()
    index, y, x, core = place()
    wb = jnp.zeros((3 * R, F), F32)
    own = jnp.zeros((R, 32), F32)
    for i in range(STEPS):
        columns = slice(i * TILE, (i + 1) * TILE)
        split = jnp.concatenate(pieces(basis_t[:, columns], 3), axis=0)
        rows = jnp.concatenate(pieces(resid[:, columns].astype(F32) + feedback[:, columns], 3), axis=0)
        rb = nt(split, rows)
        rb = rb[0:R] + rb[R : 2 * R] + rb[2 * R : 3 * R]
        own = own + (rb[:, 0:32] + rb[:, 32:64] + rb[:, 64:96])
        copies[i].wait()
        wb = wb + nn(split, held[columns, :])
        if i == 1:
            loads[3].wait()
            loads[4].wait()
        if i >= 1 and i < 7:
            for k in range(16 * (i - 1) // 6, 16 * i // 6):
                rows = slice(k * 32, (k + 1) * 32)
                g = gate[rows].astype(F32)
                unit[rows] = (hidden[rows].astype(F32) * (g / (1.0 + jnp.exp(-g)))).astype(BF)
    for place_to, block in enumerate(row_blocks(y, x, core)):
        ordered[pl.ds(place_to * 32, 32), :] = unit[pl.ds(pl.multiple_of(block * 32, 32), 32), :]
    total = wb[0:R, :] + wb[R : 2 * R, :] + wb[2 * R : 3 * R, :]
    raw3 = nt(jnp.concatenate(pieces(total, 3), axis=0), unit[...])
    raw = raw3[0:R] + raw3[R : 2 * R] + raw3[2 * R : 3 * R]
    placed = nn(jnp.concatenate(pieces(own, 3), axis=0), selection(index))
    raw_t[...] = raw + placed[0:R] + placed[R : 2 * R] + placed[2 * R : 3 * R]


def selection(index):
    spot = lax.broadcasted_iota(jnp.int32, (32, T), 1) - index * 32
    return (spot == lax.broadcasted_iota(jnp.int32, (32, T), 0)).astype(BF)


VMEM = pl.BlockSpec(memory_space=pltpu.VMEM)
ANY = pl.BlockSpec(memory_space=pl.ANY)
TOKEN = jax.ShapeDtypeStruct((8, 128), F32)


def whole(kernel, out_shape, name, operands, deps=(), flops=0, moved=0, out_specs=None, scratch=(), in_specs=None, limit=VMEM_LIMIT):
    count = len(operands)

    def body(*refs):
        kernel(*refs[:count], *refs[count + len(deps) :])

    return pl.pallas_call(
        body,
        in_specs=(in_specs or [VMEM] * count) + [ANY] * len(deps),
        out_specs=out_specs or [VMEM] * len(out_shape),
        out_shape=out_shape,
        scratch_shapes=list(scratch),
        compiler_params=params(limit),
        cost_estimate=pl.CostEstimate(flops=1000, bytes_accessed=1000, transcendentals=0),
        name=name,
    )(*operands, *deps)


def shape(*dims, dtype=F32):
    return jax.ShapeDtypeStruct(dims, dtype)


def unit_call(gate, hidden, weight, basis_t, resid, feedback):
    return whole(
        unit_kernel,
        [shape(T, F, dtype=BF), shape(T, F, dtype=BF), shape(R, T)],
        "unit_and_raw",
        (gate, hidden, weight, basis_t, resid, feedback),
        flops=2 * D * F * 192,
        moved=15_000_000,
        in_specs=[pl.BlockSpec(memory_space=pltpu.HBM)] * 6,
        limit=60 * 1024 * 1024,
        scratch=[
            pltpu.VMEM((D, F), BF),
            pltpu.VMEM((T, F), BF),
            pltpu.VMEM((T, F), BF),
            pltpu.VMEM((R, D), F32),
            pltpu.VMEM((32, D), BF),
            pltpu.VMEM((32, D), F32),
            pltpu.SemaphoreType.DMA((5,)),
            pltpu.SemaphoreType.DMA((STEPS,)),
        ],
    )


def partial_call(ordered, weight, quarter, earlier, deps):
    column = lambda i: (0, quarter * 2 + i)
    count = len(earlier) + len(deps)

    def kernel(unit, held, *refs):
        rows = pl.ds(pl.multiple_of((quarter * 2 + pl.program_id(0)) * TILE, TILE), TILE)
        product = nt(unit[...], held[rows, :])
        refs[count][...] = product[0:256].astype(BF)
        refs[count + 1][...] = product[256:512]
        refs[-1][...] = jnp.zeros((8, 128), F32)

    return pl.pallas_call(
        kernel,
        grid=(2,),
        in_specs=[VMEM, VMEM] + [ANY] * count,
        out_specs=[pl.BlockSpec((256, TILE), column)] * 2 + [pl.BlockSpec((8, 128), lambda i: (0, 0))],
        out_shape=[shape(256, D, dtype=BF), shape(256, D), TOKEN],
        input_output_aliases={2 + k: k for k in range(len(earlier))},
        compiler_params=params(),
        cost_estimate=pl.CostEstimate(flops=1000, bytes_accessed=1000, transcendentals=0),
        name="input_grad_part",
    )(ordered, weight, *earlier, *deps)


def added(a, b, deps=()):
    def kernel(a_ref, b_ref, out):
        out[...] = a_ref[...] + b_ref[...]

    return whole(kernel, [shape(*a.shape)], "raw_sum", (a, b), deps, moved=400_000)[0]


def stacked(values, deps):
    rows = values[0].shape[0]

    def kernel(*refs):
        for k, ref in enumerate(refs[:-1]):
            refs[-1][k * rows : (k + 1) * rows] = ref[...]

    return whole(kernel, [shape(len(values) * rows, D, dtype=BF)], "stack", values, deps, moved=1_300_000)[0]


def grad_start(own, come, deps):
    def kernel(own_ref, come_ref, send, kept):
        send[...] = (own_ref[0:128] + come_ref[0:128].astype(F32)).astype(BF)
        kept[...] = own_ref[128:256] + come_ref[128:256].astype(F32)

    shapes = [shape(128, D, dtype=BF), shape(128, D)]
    return whole(kernel, shapes, "input_grad_sum", (own, come), deps, moved=8_000_000)


def grad_step(kept, come, deps):
    half = kept.shape[0] // 2

    def kernel(kept_ref, come_ref, send, out):
        send[...] = (kept_ref[0:half] + come_ref[0:half].astype(F32)).astype(BF)
        out[...] = kept_ref[half:] + come_ref[half:].astype(F32)

    shapes = [shape(half, D, dtype=BF), shape(half, D)]
    return whole(kernel, shapes, "input_grad_sum", (kept, come), deps, moved=6_000_000)


def chunk_pair(right, right_next, deps):
    def kernel(a, b, out):
        out[0:1] = a[...]
        out[1:2] = b[...]

    return whole(kernel, [shape(2, R, TILE, dtype=BF)], "chunk_pair", (right, right_next), deps, moved=300_000)[0]


def eliminated(gram):
    rows = lax.broadcasted_iota(jnp.int32, (R, 2 * R), 0)
    lanes = lax.broadcasted_iota(jnp.int32, (R, 2 * R), 1)
    work = jnp.concatenate([gram, jnp.zeros((R, R), F32)], axis=1)
    work = jnp.where(lanes == rows + R, 1.0, work)
    scales = []
    for j in range(R):
        column = work[:, j : j + 1]
        pivot = column[j : j + 1, :]
        row = work[j : j + 1, :]
        scales.append(row * lax.rsqrt(pivot))
        work = work - jnp.where(rows[:, 0:1] > j, column, 0.0) * (row / pivot)
    return jnp.concatenate(scales, axis=0)[:, R:]


def exact(op, a, b):
    a1, a2, a3 = pieces(a, 3)
    b1, b2, b3 = pieces(b, 3)
    low = op(a1, b3) + op(a2, b2) + op(a3, b1)
    return op(a1, b1) + (op(a1, b2) + op(a2, b1) + low)


def basis_kernel(raw_a, raw_b, unit, z, left, left_t):
    index, _, _, _ = place()
    raw = raw_a[...] + raw_b[...]
    inverse = eliminated(exact(nt, raw, raw))
    parts = jnp.concatenate(pieces(exact(nn, inverse, raw), 3), axis=0)
    z3 = nn(parts, unit[...])
    z[...] = jnp.concatenate(pieces(z3[0:R] + z3[R : 2 * R] + z3[2 * R : 3 * R], 2), axis=0)
    select = selection(index)
    own3 = nt(select, parts)
    left[...] = own3[:, 0:R] + own3[:, R : 2 * R] + own3[:, 2 * R : 3 * R]
    own_t = nt(parts, select)
    left_t[...] = own_t[0:R] + own_t[R : 2 * R] + own_t[2 * R : 3 * R]


def basis_call(raw_a, raw_b, unit, deps):
    return whole(
        basis_kernel,
        [shape(2 * R, F, dtype=BF), shape(32, R), shape(R, 32)],
        "left_factor",
        (raw_a, raw_b, unit),
        deps,
        flops=7_000_000_000,
        moved=2_000_000,
    )


def factor_kernel(z, left_t, weight, resid, feedback, own_out, other_out):
    _, _, x, core = place()
    l1, l2 = pieces(left_t[...], 2)
    for step in range(STEPS):
        columns = slice(step * TILE, (step + 1) * TILE)
        both = nt(z[...], weight[columns, :])
        value = both[0:R] + both[R : 2 * R]
        r1, r2 = pieces(resid[:, columns].astype(F32) + feedback[:, columns], 2)
        value = value + (nn(l1, r1) + (nn(l1, r2) + nn(l2, r1)))
        c = step // 4
        apart = xor_x(step % 4, x)
        spot = jnp.where(apart == 0, 3, jnp.where(apart == 2, 0, jnp.where(apart == 1 + 2 * c, 1, 2)))

        @pl.when(core == c)
        def _():
            own_out[spot] = value

        @pl.when(core != c)
        def _():
            other_out[spot] = value.astype(BF)


def factor_call(z, left_t, weight, resid, feedback, deps):
    return whole(
        factor_kernel,
        [shape(4, R, TILE), shape(4, R, TILE, dtype=BF)],
        "right_factor",
        (z, left_t, weight, resid, feedback),
        deps,
        flops=2 * D * F * 192,
        moved=12_000_000,
    )


def right_step(total, come, deps):
    keep = total.shape[0] // 2

    def kernel(total_ref, come_ref, send, kept):
        value = total_ref[...] + come_ref[...].astype(F32)
        send[...] = value[0:keep].astype(BF)
        kept[...] = value[keep:]

    shapes = [shape(keep, R, TILE, dtype=BF), shape(keep, R, TILE)]
    return whole(kernel, shapes, "right_sum", (total, come), deps, moved=1_500_000)


def right_last(kept, come, deps, dtype=F32):
    def kernel(kept_ref, come_ref, out):
        out[...] = (kept_ref[...] + come_ref[...]).astype(out.dtype)

    return whole(kernel, [shape(1, R, TILE, dtype=dtype)], "right_sum", (kept, come), deps, moved=500_000)[0]


def grad_call(tokens, ordered, quarter, earlier, deps):
    count = len(earlier) + len(deps)
    ins = len(tokens)

    def kernel(*refs):
        unit, out, token, held, sems = refs[ins], *refs[ins + 1 + count :]
        copies = []
        for k in (0, 1):
            start = (quarter * 2 + k) * TILE
            columns = slice(start, start + TILE)
            blocks = []
            for near, far in (refs[0:2], refs[2:4]):
                for group in (3, 1, 2, 0):
                    rows = slice(group * 32, group * 32 + 32)
                    blocks += [far[rows, columns], near[rows, columns]]
            held[k] = tn(jnp.concatenate(blocks, axis=0), unit[...]).astype(BF)
            copies.append(pltpu.make_async_copy(held.at[k], out.at[pl.ds(start, TILE)], sems.at[k]))
            copies[-1].start()
        token[...] = jnp.zeros((8, 128), F32)
        for copy in copies:
            copy.wait()

    return pl.pallas_call(
        kernel,
        in_specs=[VMEM] * (ins + 1) + [ANY] * count,
        out_specs=[ANY, VMEM],
        out_shape=[shape(D, F, dtype=BF), TOKEN],
        scratch_shapes=[pltpu.VMEM((2, TILE, F), BF), pltpu.SemaphoreType.DMA((2,))],
        input_output_aliases={ins + 1: 0} if earlier else {},
        compiler_params=params(),
        cost_estimate=pl.CostEstimate(flops=1000, bytes_accessed=1000, transcendentals=0),
        name="weight_grad_part",
    )(*tokens, ordered, *earlier, *deps)


def final_kernel(*refs):
    chunks, (left, left_next, resid, feedback, mine, partner, out, received) = refs[:8], refs[8:]
    _, _, x, core = place()
    l3 = jnp.concatenate(pieces(left[...], 2), axis=0)
    n3 = jnp.concatenate(pieces(left_next[...], 2), axis=0)
    for h in (0, 1):
        c = core if h == 0 else 1 - core
        first, second = 1 + 2 * c, 3 - 2 * c
        for k, xx in enumerate((xor_x(x, 2), xor_x(x, first), xor_x(x, second), x)):
            columns = pl.ds(pl.multiple_of((c * 4 + xx) * TILE, 128), TILE)
            chunk = chunks[h * 4 + k]
            here = nn(l3, chunk[0])
            there = nn(n3, chunk[1])
            merged = resid[:, columns].astype(F32) + feedback[:, columns]
            merged = merged + (mine[:, columns] + partner[:, columns].astype(F32))
            out[:, columns] = merged - (here[0:32] + here[32:64])
            received[:, columns] = there[0:32] + there[32:64]


def final_call(chunks, left, left_next, resid, feedback, mine, partner):
    vmem = pl.BlockSpec(memory_space=pltpu.VMEM)
    return pl.pallas_call(
        final_kernel,
        in_specs=[vmem] * 14,
        out_specs=[vmem, vmem],
        out_shape=[jax.ShapeDtypeStruct((32, D), F32)] * 2,
        compiler_params=params(),
        cost_estimate=pl.CostEstimate(flops=1000, bytes_accessed=1000, transcendentals=0),
        name="feedback_and_received",
    )(*chunks, left, left_next, resid, feedback, mine, partner)


def sent(value, move):
    pairs = []
    for index in range(16):
        y, x, core = move(index // 8, (index // 2) % 4, index % 2)
        pairs.append((index, y * 8 + x * 2 + core))
    return lax.ppermute(value, "fsdp", pairs)


def to_core(value):
    return sent(value, lambda y, x, c: (y, x, 1 - c))


def to_first(value):
    return sent(value, lambda y, x, c: (y, x ^ (1 + 2 * c), c))


def to_second(value):
    return sent(value, lambda y, x, c: (y, x ^ (3 - 2 * c), c))


def to_far(value):
    return sent(value, lambda y, x, c: (y, x ^ 2, c))


def to_y(value):
    return sent(value, lambda y, x, c: (1 - y, x, c))


def to_previous(value):
    return lax.ppermute(value, "section", [(s, s - 1) for s in range(1, 8)])


def on_device(activations, gate_preact, hidden_grad, up_weight, resid_grad, feedback, start_basis):
    acts, resid, fb = activations[0], resid_grad[0], feedback[0]
    basis_t = jnp.swapaxes(start_basis[0], 0, 1)

    weight = up_weight[0]
    moved = to_first(acts), to_second(acts), to_far(acts)
    unit, ordered, raw = unit_call(gate_preact[0], hidden_grad[0], weight, basis_t, resid, fb)

    raw = added(raw, to_core(raw))
    come = to_first(raw)
    *parts, token = partial_call(ordered, weight, 0, (), (raw,))
    *parts, token = partial_call(ordered, weight, 1, parts, (token,))
    raw = added(raw, come, (token, *moved))
    come = to_second(raw)
    *parts, token = partial_call(ordered, weight, 2, parts, (raw,))
    other, own, token = partial_call(ordered, weight, 3, parts, (token,))
    raw = added(raw, come, (token,))
    come = to_y(raw)
    come_grad = to_core(other)
    near = stacked((acts, *moved), (raw,))
    far = to_y(near)

    send, grad_kept = grad_start(own, come_grad, (come,))
    grad_first = to_first(send)
    z, left, left_t = basis_call(raw, come, unit, (send,))
    left_next = to_previous(left)
    own, other = factor_call(z, left_t, weight, resid, fb, ())

    come = to_core(other)
    send, kept = right_step(own, come, (grad_first,))
    come = to_first(send)
    send, kept = right_step(kept, come, (left_next,))
    come = to_second(send)
    far = stacked((far,), (kept,))
    tokens = [to_core(near), to_core(far), near, far]
    half_sum = right_last(kept, come, ())
    come = to_y(half_sum)
    send, grad_kept = grad_step(grad_kept, grad_first, (half_sum,))
    grad_second = to_second(send)
    grad, token = grad_call(tokens, ordered, 0, (), (send,))
    grad, token = grad_call(tokens, ordered, 1, (grad,), (token,))
    right = right_last(half_sum, come, (token,), BF)
    right_next = to_previous(right)
    send, mine = grad_step(grad_kept, grad_second, (right,))
    partner = to_y(send)
    grad, token = grad_call(tokens, ordered, 2, (grad,), (send,))
    weight_grad, token = grad_call(tokens, ordered, 3, (grad,), (token,))

    both = chunk_pair(right, right_next, (token,))
    both_first, both_second, both_far = to_first(both), to_second(both), to_far(both)
    own_chunks = [both_far, both_first, both_second, both]
    chunks = own_chunks + [to_core(value) for value in own_chunks]

    new_feedback, received = final_call(chunks, left, left_next, resid, fb, mine, partner)
    return (weight_grad[None], new_feedback[None], received[None])


def solution(mesh):
    return jax.shard_map(
        on_device,
        mesh=mesh,
        in_specs=(
            P("section", "fsdp", None),
            P("section", None, "fsdp"),
            P("section", None, "fsdp"),
            P("section", None, "fsdp"),
            P("section", "fsdp", None),
            P("section", "fsdp", None),
            P("section", None, None),
        ),
        out_specs=(
            P("section", None, "fsdp"),
            P("section", "fsdp", None),
            P("section", "fsdp", None),
        ),
        check_vma=False,
    )
```

```python
import jax
import jax.numpy as jnp
from jax import lax
from jax.experimental import pallas as pl
from jax.experimental.pallas import tpu as pltpu
from jax.sharding import PartitionSpec as P

D = 5120
F = 896
R = 64
T = 512
TILE = 640
STEPS = D // TILE
BF = jnp.bfloat16
F32 = jnp.float32
VMEM_LIMIT = 24 * 1024 * 1024


def params(limit=VMEM_LIMIT):
    return pltpu.CompilerParams(vmem_limit_bytes=limit)


def place():
    index = lax.axis_index("fsdp")
    y, x, core = index // 8, (index // 2) % 4, index % 2
    return index, y, x, core


def xor_x(x, mask):
    return x + mask - 2 * (x & mask)


def pieces(value, count):
    out = []
    for _ in range(count):
        part = value.astype(BF)
        out.append(part)
        value = value - part.astype(F32)
    return out


def nn(a, b):
    return lax.dot_general(a, b, (((1,), (0,)), ((), ())), preferred_element_type=F32)


def nt(a, b):
    return lax.dot_general(a, b, (((1,), (1,)), ((), ())), preferred_element_type=F32)


def tn(a, b):
    return lax.dot_general(a, b, (((0,), (0,)), ((), ())), preferred_element_type=F32)


def row_blocks(y, x, core):
    out = []
    for c in (1 - core, core):
        first, second = 1 + 2 * c, 3 - 2 * c
        for xx in (xor_x(x, 2), xor_x(x, first), xor_x(x, second), x):
            for yy in (1 - y, y):
                out.append(yy * 8 + xx * 2 + c)
    return out


def unit_kernel(gate, hidden, weight, basis_t, resid, feedback, unit, ordered, raw_t):
    index, y, x, core = place()
    wb = jnp.zeros((3 * R, F), F32)
    own = jnp.zeros((R, 32), F32)
    for i in range(STEPS):
        columns = slice(i * TILE, (i + 1) * TILE)
        split = jnp.concatenate(pieces(basis_t[:, columns], 3), axis=0)
        rows = jnp.concatenate(pieces(resid[:, columns].astype(F32) + feedback[:, columns], 3), axis=0)
        rb = nt(split, rows)
        rb = rb[0:R] + rb[R : 2 * R] + rb[2 * R : 3 * R]
        own = own + (rb[:, 0:32] + rb[:, 32:64] + rb[:, 64:96])
        wb = wb + nn(split, weight[columns, :])
        for k in range(2 * i, 2 * i + 2):
            rows = slice(k * 32, (k + 1) * 32)
            g = gate[rows].astype(F32)
            unit[rows] = (hidden[rows].astype(F32) * (g / (1.0 + jnp.exp(-g)))).astype(BF)
    for place_to, block in enumerate(row_blocks(y, x, core)):
        ordered[pl.ds(place_to * 32, 32), :] = unit[pl.ds(pl.multiple_of(block * 32, 32), 32), :]
    total = wb[0:R, :] + wb[R : 2 * R, :] + wb[2 * R : 3 * R, :]
    raw3 = nt(jnp.concatenate(pieces(total, 3), axis=0), unit[...])
    raw = raw3[0:R] + raw3[R : 2 * R] + raw3[2 * R : 3 * R]
    placed = nn(jnp.concatenate(pieces(own, 3), axis=0), selection(index))
    raw_t[...] = raw + placed[0:R] + placed[R : 2 * R] + placed[2 * R : 3 * R]


def selection(index):
    spot = lax.broadcasted_iota(jnp.int32, (32, T), 1) - index * 32
    return (spot == lax.broadcasted_iota(jnp.int32, (32, T), 0)).astype(BF)


VMEM = pl.BlockSpec(memory_space=pltpu.VMEM)
ANY = pl.BlockSpec(memory_space=pl.ANY)
TOKEN = jax.ShapeDtypeStruct((8, 128), F32)


def whole(kernel, out_shape, name, operands, deps=(), flops=1000, out_specs=None, scratch=(), in_specs=None, limit=VMEM_LIMIT):
    count = len(operands)

    def body(*refs):
        kernel(*refs[:count], *refs[count + len(deps) :])

    return pl.pallas_call(
        body,
        in_specs=(in_specs or [VMEM] * count) + [ANY] * len(deps),
        out_specs=out_specs or [VMEM] * len(out_shape),
        out_shape=out_shape,
        scratch_shapes=list(scratch),
        compiler_params=params(limit),
        cost_estimate=pl.CostEstimate(flops=flops, bytes_accessed=1000, transcendentals=0),
        name=name,
    )(*operands, *deps)


def shape(*dims, dtype=F32):
    return jax.ShapeDtypeStruct(dims, dtype)


def unit_call(gate, hidden, weight, basis_t, resid, feedback, deps):
    return whole(
        unit_kernel,
        [shape(T, F, dtype=BF), shape(T, F, dtype=BF), shape(R, T)],
        "unit_and_raw",
        (gate, hidden, weight, basis_t, resid, feedback),
        deps,
        flops=20_000_000_000,
    )


def partial_call(ordered, weight, quarter, earlier, deps):
    column = lambda i: (0, quarter * 2 + i)
    count = len(earlier) + len(deps)

    def kernel(unit, held, *refs):
        rows = pl.ds(pl.multiple_of((quarter * 2 + pl.program_id(0)) * TILE, TILE), TILE)
        product = nt(unit[...], held[rows, :])
        refs[count][...] = product[0:256].astype(BF)
        refs[count + 1][...] = product[256:512]
        refs[-1][...] = jnp.zeros((8, 128), F32)

    return pl.pallas_call(
        kernel,
        grid=(2,),
        in_specs=[VMEM, VMEM] + [ANY] * count,
        out_specs=[pl.BlockSpec((256, TILE), column)] * 2 + [pl.BlockSpec((8, 128), lambda i: (0, 0))],
        out_shape=[shape(256, D, dtype=BF), shape(256, D), TOKEN],
        input_output_aliases={2 + k: k for k in range(len(earlier))},
        compiler_params=params(),
        cost_estimate=pl.CostEstimate(flops=1000, bytes_accessed=1000, transcendentals=0),
        name="input_grad_part",
    )(ordered, weight, *earlier, *deps)


def added(a, b, deps=()):
    def kernel(a_ref, b_ref, out):
        out[...] = a_ref[...] + b_ref[...]

    return whole(kernel, [shape(*a.shape)], "raw_sum", (a, b), deps)[0]


def stacked(values, deps):
    rows = values[0].shape[0]

    def kernel(*refs):
        for k, ref in enumerate(refs[:-1]):
            refs[-1][k * rows : (k + 1) * rows] = ref[...]

    return whole(kernel, [shape(len(values) * rows, D, dtype=BF)], "stack", values, deps)[0]


def grad_start(own, come, deps):
    def kernel(own_ref, come_ref, send, kept):
        send[...] = (own_ref[0:128] + come_ref[0:128].astype(F32)).astype(BF)
        kept[...] = own_ref[128:256] + come_ref[128:256].astype(F32)

    shapes = [shape(128, D, dtype=BF), shape(128, D)]
    return whole(kernel, shapes, "input_grad_sum", (own, come), deps)


def grad_step(kept, come, deps):
    half = kept.shape[0] // 2

    def kernel(kept_ref, come_ref, send, out):
        send[...] = (kept_ref[0:half] + come_ref[0:half].astype(F32)).astype(BF)
        out[...] = kept_ref[half:] + come_ref[half:].astype(F32)

    shapes = [shape(half, D, dtype=BF), shape(half, D)]
    return whole(kernel, shapes, "input_grad_sum", (kept, come), deps)


def chunk_pair(half, come, ahead, ahead_far, deps):
    def kernel(a, b, c, d, out):
        out[0:1] = (a[...] + b[...].astype(F32)).astype(BF)
        out[1:2] = (c[...] + d[...].astype(F32)).astype(BF)

    return whole(kernel, [shape(2, R, TILE, dtype=BF)], "chunk_pair", (half, come, ahead, ahead_far), deps)[0]


def copied_whole(value, deps, flops=1000):
    def kernel(ref, out):
        out[...] = ref[...]

    return whole(kernel, [shape(*value.shape, dtype=value.dtype)], "copied", (value,), deps, flops)[0]


def eliminated(gram):
    rows = lax.broadcasted_iota(jnp.int32, (R, 2 * R), 0)
    lanes = lax.broadcasted_iota(jnp.int32, (R, 2 * R), 1)
    work = jnp.concatenate([gram, jnp.zeros((R, R), F32)], axis=1)
    work = jnp.where(lanes == rows + R, 1.0, work)
    scales = []
    for j in range(0, R, 8):
        columns = [jnp.broadcast_to(work[:, j + k : j + k + 1], (R, 2 * R)) for k in range(8)]
        block = [work[j + k : j + k + 1, :] for k in range(8)]
        for k in range(8):
            pivot = columns[k][j + k : j + k + 1, :]
            inverse = 1.0 / pivot
            scales.append(block[k] * lax.rsqrt(pivot))
            row = block[k] * inverse
            for m in range(k + 1, 8):
                factor = columns[k][j + m : j + m + 1, :]
                columns[m] = columns[m] - columns[k] * (factor * inverse)
                block[m] = block[m] - row * factor
            work = work - jnp.where(rows > j + k, columns[k], 0.0) * row
    return jnp.concatenate(scales, axis=0)[:, R:]


def exact(op, a, b):
    a1, a2, a3 = pieces(a, 3)
    b1, b2, b3 = pieces(b, 3)
    low = op(a1, b3) + op(a2, b2) + op(a3, b1)
    return op(a1, b1) + (op(a1, b2) + op(a2, b1) + low)


def basis_kernel(raw_a, raw_b, unit, z, left, left_t):
    index, _, _, _ = place()
    raw = raw_a[...] + raw_b[...]
    inverse = eliminated(exact(nt, raw, raw))
    parts = jnp.concatenate(pieces(exact(nn, inverse, raw), 3), axis=0)
    z3 = nn(parts, unit[...])
    z[...] = jnp.concatenate(pieces(z3[0:R] + z3[R : 2 * R] + z3[2 * R : 3 * R], 2), axis=0)
    select = selection(index)
    own3 = nt(select, parts)
    left[...] = own3[:, 0:R] + own3[:, R : 2 * R] + own3[:, 2 * R : 3 * R]
    own_t = nt(parts, select)
    left_t[...] = own_t[0:R] + own_t[R : 2 * R] + own_t[2 * R : 3 * R]


def basis_call(raw_a, raw_b, unit, deps):
    return whole(
        basis_kernel,
        [shape(2 * R, F, dtype=BF), shape(32, R), shape(R, 32)],
        "left_factor",
        (raw_a, raw_b, unit),
        deps,

    )


def factor_kernel(z, left_t, weight, resid, feedback, own_out, other_out):
    _, _, x, core = place()
    l1, l2 = pieces(left_t[...], 2)
    for step in range(STEPS):
        columns = slice(step * TILE, (step + 1) * TILE)
        both = nt(z[...], weight[columns, :])
        value = both[0:R] + both[R : 2 * R]
        r1, r2 = pieces(resid[:, columns].astype(F32) + feedback[:, columns], 2)
        value = value + (nn(l1, r1) + (nn(l1, r2) + nn(l2, r1)))
        c = step // 4
        apart = xor_x(step % 4, x)
        spot = jnp.where(apart == 0, 3, jnp.where(apart == 2, 0, jnp.where(apart == 1 + 2 * c, 1, 2)))

        @pl.when(core == c)
        def _():
            own_out[spot] = value

        @pl.when(core != c)
        def _():
            other_out[spot] = value.astype(BF)


def factor_call(z, left_t, weight, resid, feedback, deps):
    return whole(
        factor_kernel,
        [shape(4, R, TILE), shape(4, R, TILE, dtype=BF)],
        "right_factor",
        (z, left_t, weight, resid, feedback),
        deps,
    )


def right_step(total, come, deps):
    keep = total.shape[0] // 2

    def kernel(total_ref, come_ref, send, kept):
        value = total_ref[...] + come_ref[...].astype(F32)
        send[...] = value[0:keep].astype(BF)
        kept[...] = value[keep:]

    shapes = [shape(keep, R, TILE, dtype=BF), shape(keep, R, TILE)]
    return whole(kernel, shapes, "right_sum", (total, come), deps)


def right_sum(total, come, deps):
    def kernel(total_ref, come_ref, send, kept):
        value = total_ref[...] + come_ref[...].astype(F32)
        send[...] = value.astype(BF)
        kept[...] = value

    shapes = [shape(*total.shape, dtype=BF), shape(*total.shape)]
    return whole(kernel, shapes, "right_sum", (total, come), deps)


def grad_call(tokens, ordered, quarter, earlier, deps):
    count = len(earlier) + len(deps)
    ins = len(tokens)

    def kernel(*refs):
        unit, out, token, held, sems = refs[ins], *refs[ins + 1 + count :]
        copies = []
        for k in (0, 1):
            start = (quarter * 2 + k) * TILE
            columns = slice(start, start + TILE)
            blocks = []
            for near, far in (refs[0:2], refs[2:4]):
                for group in (3, 1, 2, 0):
                    rows = slice(group * 32, group * 32 + 32)
                    blocks += [far[rows, columns], near[rows, columns]]
            held[k] = tn(jnp.concatenate(blocks, axis=0), unit[...]).astype(BF)
            copies.append(pltpu.make_async_copy(held.at[k], out.at[pl.ds(start, TILE)], sems.at[k]))
            copies[-1].start()
        token[...] = jnp.zeros((8, 128), F32)
        for copy in copies:
            copy.wait()

    return pl.pallas_call(
        kernel,
        in_specs=[VMEM] * (ins + 1) + [ANY] * count,
        out_specs=[ANY, VMEM],
        out_shape=[shape(D, F, dtype=BF), TOKEN],
        scratch_shapes=[pltpu.VMEM((2, TILE, F), BF), pltpu.SemaphoreType.DMA((2,))],
        input_output_aliases={ins + 1: 0} if earlier else {},
        compiler_params=params(),
        cost_estimate=pl.CostEstimate(flops=1000, bytes_accessed=1000, transcendentals=0),
        name="weight_grad_part",
    )(*tokens, ordered, *earlier, *deps)


def final_kernel(*refs):
    chunks, (left, left_next, resid, feedback, mine, partner, out, received) = refs[:8], refs[8:]
    _, _, x, core = place()
    l3 = jnp.concatenate(pieces(left[...], 2), axis=0)
    n3 = jnp.concatenate(pieces(left_next[...], 2), axis=0)
    for h in (0, 1):
        c = core if h == 0 else 1 - core
        first, second = 1 + 2 * c, 3 - 2 * c
        for k, xx in enumerate((xor_x(x, 2), xor_x(x, first), xor_x(x, second), x)):
            columns = pl.ds(pl.multiple_of((c * 4 + xx) * TILE, 128), TILE)
            chunk = chunks[h * 4 + k]
            here = nn(l3, chunk[0])
            there = nn(n3, chunk[1])
            merged = resid[:, columns].astype(F32) + feedback[:, columns]
            merged = merged + (mine[:, columns] + partner[:, columns].astype(F32))
            out[:, columns] = merged - (here[0:32] + here[32:64])
            received[:, columns] = there[0:32] + there[32:64]


def final_call(chunks, left, left_next, resid, feedback, mine, partner):
    vmem = pl.BlockSpec(memory_space=pltpu.VMEM)
    return pl.pallas_call(
        final_kernel,
        in_specs=[vmem] * 14,
        out_specs=[vmem, vmem],
        out_shape=[jax.ShapeDtypeStruct((32, D), F32)] * 2,
        compiler_params=params(),
        cost_estimate=pl.CostEstimate(flops=1000, bytes_accessed=1000, transcendentals=0),
        name="feedback_and_received",
    )(*chunks, left, left_next, resid, feedback, mine, partner)


def sent(value, move):
    pairs = []
    for index in range(16):
        y, x, core = move(index // 8, (index // 2) % 4, index % 2)
        pairs.append((index, y * 8 + x * 2 + core))
    return lax.ppermute(value, "fsdp", pairs)


def to_core(value):
    return sent(value, lambda y, x, c: (y, x, 1 - c))


def to_first(value):
    return sent(value, lambda y, x, c: (y, x ^ (1 + 2 * c), c))


def to_second(value):
    return sent(value, lambda y, x, c: (y, x ^ (3 - 2 * c), c))


def to_far(value):
    return sent(value, lambda y, x, c: (y, x ^ 2, c))


def to_y(value):
    return sent(value, lambda y, x, c: (1 - y, x, c))


def to_previous(value):
    return lax.ppermute(value, "section", [(s, s - 1) for s in range(1, 8)])


def to_previous_second(value):
    pairs = []
    for s in range(1, 8):
        for i in range(16):
            pairs.append((s * 16 + i, (s - 1) * 16 + (i ^ (2 * (3 - 2 * (i % 2))))))
    return lax.ppermute(value, ("section", "fsdp"), pairs)


def on_device(activations, gate_preact, hidden_grad, up_weight, resid_grad, feedback, start_basis):
    acts, resid, fb = activations[0], resid_grad[0], feedback[0]
    basis_t = jnp.swapaxes(start_basis[0], 0, 1)

    weight = up_weight[0]
    first_acts = copied_whole(acts, (), 20_000_000_000)
    moved_first, moved_second, acts_y = to_first(first_acts), to_second(first_acts), to_y(first_acts)
    unit, ordered, raw = unit_call(gate_preact[0], hidden_grad[0], weight, basis_t, resid, fb, ())

    come = to_core(raw)
    sent_first, sent_second = stacked((acts_y,), (raw, moved_second)), stacked((acts_y, moved_first), (raw, moved_second))
    gone_first, gone_second = to_first(sent_first), to_second(sent_second)
    *parts, token = partial_call(ordered, weight, 0, (), (raw,))
    raw = added(raw, come, (token,))
    come = to_y(raw)
    *parts, token = partial_call(ordered, weight, 1, parts, (raw,))
    raw = added(raw, come, (token,))
    come = to_first(raw)
    *parts, token = partial_call(ordered, weight, 2, parts, (raw,))
    other, own, token = partial_call(ordered, weight, 3, parts, (token,))
    raw = added(raw, come, (token, gone_first, gone_second))
    gone_far = to_first(gone_second[0:32])
    near = stacked((acts, moved_first, moved_second, gone_second[32:64]), (raw,))
    come = to_second(raw)
    come_grad = to_core(stacked((other,), (raw,)))

    far = stacked((acts_y, gone_first, gone_second[0:32], gone_far), (come,))
    send, grad_kept = grad_start(own, come_grad, (come, far))
    grad_first = to_first(send)
    z, left, left_t = basis_call(raw, come, unit, (send,))
    left_next = to_previous(left)
    own, other = factor_call(z, left_t, weight, resid, fb, ())

    come = to_core(other)
    send, kept = right_step(own, come, ())
    come = to_first(send)
    tokens = [to_core(near), to_core(far), near, far]
    grad, token = grad_call(tokens, ordered, 0, (), (kept,))
    send, kept = right_sum(kept, come, (left_next, token))
    come = to_y(send)
    send, grad_kept = grad_step(grad_kept, grad_first, (kept,))
    grad_second = to_second(send)
    grad, token = grad_call(tokens, ordered, 1, (grad,), (send,))
    grad, token = grad_call(tokens, ordered, 2, (grad,), (token,))
    send, kept = right_step(kept, come, (token,))
    come, ahead, ahead_far = to_second(send), to_previous(kept), to_previous_second(send)
    weight_grad, token = grad_call(tokens, ordered, 3, (grad,), (kept,))
    both = chunk_pair(kept, come, ahead, ahead_far, (token,))
    send, mine = grad_step(grad_kept, grad_second, (both,))
    partner = to_y(send)
    both_first, both_second, both_far = to_first(both), to_second(both), to_far(both)
    own_chunks = [both_far, both_first, both_second, both]
    chunks = own_chunks + [to_core(value) for value in own_chunks]

    new_feedback, received = final_call(chunks, left, left_next, resid, fb, mine, partner)
    return (weight_grad[None], new_feedback[None], received[None])


def solution(mesh):
    return jax.shard_map(
        on_device,
        mesh=mesh,
        in_specs=(
            P("section", "fsdp", None),
            P("section", None, "fsdp"),
            P("section", None, "fsdp"),
            P("section", None, "fsdp"),
            P("section", "fsdp", None),
            P("section", "fsdp", None),
            P("section", None, None),
        ),
        out_specs=(
            P("section", None, "fsdp"),
            P("section", "fsdp", None),
            P("section", "fsdp", None),
        ),
        check_vma=False,
    )
```

```python
import jax
import jax.numpy as jnp
from jax import lax
from jax.experimental import pallas as pl
from jax.experimental.pallas import tpu as pltpu
from jax.sharding import PartitionSpec as P

D = 5120
F = 896
R = 64
T = 512
TILE = 640
STEPS = D // TILE
BF = jnp.bfloat16
F32 = jnp.float32
VMEM_LIMIT = 24 * 1024 * 1024


def params(limit=VMEM_LIMIT):
    return pltpu.CompilerParams(vmem_limit_bytes=limit)


def place():
    index = lax.axis_index("fsdp")
    y, x, core = index // 8, (index // 2) % 4, index % 2
    return index, y, x, core


def xor_x(x, mask):
    return x + mask - 2 * (x & mask)


def pieces(value, count):
    out = []
    for _ in range(count):
        part = value.astype(BF)
        out.append(part)
        value = value - part.astype(F32)
    return out


def nn(a, b):
    return lax.dot_general(a, b, (((1,), (0,)), ((), ())), preferred_element_type=F32)


def nt(a, b):
    return lax.dot_general(a, b, (((1,), (1,)), ((), ())), preferred_element_type=F32)


def tn(a, b):
    return lax.dot_general(a, b, (((0,), (0,)), ((), ())), preferred_element_type=F32)


def row_blocks(y, x, core):
    out = []
    for c in (1 - core, core):
        first, second = 1 + 2 * c, 3 - 2 * c
        for xx in (xor_x(x, 2), xor_x(x, first), xor_x(x, second), x):
            for yy in (1 - y, y):
                out.append(yy * 8 + xx * 2 + c)
    return out


def unit_kernel(gate, hidden, weight, basis_t, resid, feedback, unit, ordered, raw_t):
    index, y, x, core = place()
    wb = jnp.zeros((3 * R, F), F32)
    own = jnp.zeros((R, 32), F32)
    for i in range(STEPS):
        columns = slice(i * TILE, (i + 1) * TILE)
        split = jnp.concatenate(pieces(basis_t[:, columns], 3), axis=0)
        rows = jnp.concatenate(pieces(resid[:, columns].astype(F32) + feedback[:, columns], 3), axis=0)
        rb = nt(split, rows)
        rb = rb[0:R] + rb[R : 2 * R] + rb[2 * R : 3 * R]
        own = own + (rb[:, 0:32] + rb[:, 32:64] + rb[:, 64:96])
        wb = wb + nn(split, weight[columns, :])
        for k in range(2 * i, 2 * i + 2):
            rows = slice(k * 32, (k + 1) * 32)
            g = gate[rows].astype(F32)
            unit[rows] = (hidden[rows].astype(F32) * (g / (1.0 + jnp.exp(-g)))).astype(BF)
    for place_to, block in enumerate(row_blocks(y, x, core)):
        ordered[pl.ds(place_to * 32, 32), :] = unit[pl.ds(pl.multiple_of(block * 32, 32), 32), :]
    total = wb[0:R, :] + wb[R : 2 * R, :] + wb[2 * R : 3 * R, :]
    raw3 = nt(jnp.concatenate(pieces(total, 3), axis=0), unit[...])
    raw = raw3[0:R] + raw3[R : 2 * R] + raw3[2 * R : 3 * R]
    placed = nn(jnp.concatenate(pieces(own, 3), axis=0), selection(index))
    raw_t[...] = raw + placed[0:R] + placed[R : 2 * R] + placed[2 * R : 3 * R]


def selection(index):
    spot = lax.broadcasted_iota(jnp.int32, (32, T), 1) - index * 32
    return (spot == lax.broadcasted_iota(jnp.int32, (32, T), 0)).astype(BF)


VMEM = pl.BlockSpec(memory_space=pltpu.VMEM)
ANY = pl.BlockSpec(memory_space=pl.ANY)
TOKEN = jax.ShapeDtypeStruct((8, 128), F32)


def whole(kernel, out_shape, name, operands, deps=(), flops=1000, out_specs=None, scratch=(), in_specs=None, limit=VMEM_LIMIT):
    count = len(operands)

    def body(*refs):
        kernel(*refs[:count], *refs[count + len(deps) :])

    return pl.pallas_call(
        body,
        in_specs=(in_specs or [VMEM] * count) + [ANY] * len(deps),
        out_specs=out_specs or [VMEM] * len(out_shape),
        out_shape=out_shape,
        scratch_shapes=list(scratch),
        compiler_params=params(limit),
        cost_estimate=pl.CostEstimate(flops=flops, bytes_accessed=1000, transcendentals=0),
        name=name,
    )(*operands, *deps)


def shape(*dims, dtype=F32):
    return jax.ShapeDtypeStruct(dims, dtype)


def unit_call(gate, hidden, weight, basis_t, resid, feedback, deps):
    return whole(
        unit_kernel,
        [shape(T, F, dtype=BF), shape(T, F, dtype=BF), shape(R, T)],
        "unit_and_raw",
        (gate, hidden, weight, basis_t, resid, feedback),
        deps,
        flops=20_000_000_000,
    )


def partial_call(ordered, weight, quarter, earlier, deps):
    column = lambda i: (0, quarter * 2 + i)
    count = len(earlier) + len(deps)

    def kernel(unit, held, *refs):
        rows = pl.ds(pl.multiple_of((quarter * 2 + pl.program_id(0)) * TILE, TILE), TILE)
        product = nt(unit[...], held[rows, :])
        refs[count][...] = product[0:256].astype(BF)
        refs[count + 1][...] = product[256:512]
        refs[-1][...] = jnp.zeros((8, 128), F32)

    return pl.pallas_call(
        kernel,
        grid=(2,),
        in_specs=[VMEM, VMEM] + [ANY] * count,
        out_specs=[pl.BlockSpec((256, TILE), column)] * 2 + [pl.BlockSpec((8, 128), lambda i: (0, 0))],
        out_shape=[shape(256, D, dtype=BF), shape(256, D), TOKEN],
        input_output_aliases={2 + k: k for k in range(len(earlier))},
        compiler_params=params(),
        cost_estimate=pl.CostEstimate(flops=1000, bytes_accessed=1000, transcendentals=0),
        name="input_grad_part",
    )(ordered, weight, *earlier, *deps)


def added(a, b, deps=()):
    def kernel(a_ref, b_ref, out):
        out[...] = a_ref[...] + b_ref[...]

    return whole(kernel, [shape(*a.shape)], "raw_sum", (a, b), deps)[0]


def stacked(values, deps):
    rows = values[0].shape[0]

    def kernel(*refs):
        for k, ref in enumerate(refs[:-1]):
            refs[-1][k * rows : (k + 1) * rows] = ref[...]

    return whole(kernel, [shape(len(values) * rows, D, dtype=BF)], "stack", values, deps)[0]


def grad_start(own, come, deps):
    def kernel(own_ref, come_ref, send, kept):
        send[...] = (own_ref[0:128] + come_ref[0:128].astype(F32)).astype(BF)
        kept[...] = own_ref[128:256] + come_ref[128:256].astype(F32)

    shapes = [shape(128, D, dtype=BF), shape(128, D)]
    return whole(kernel, shapes, "input_grad_sum", (own, come), deps)


def grad_step(kept, come, deps):
    half = kept.shape[0] // 2

    def kernel(kept_ref, come_ref, send, out):
        send[...] = (kept_ref[0:half] + come_ref[0:half].astype(F32)).astype(BF)
        out[...] = kept_ref[half:] + come_ref[half:].astype(F32)

    shapes = [shape(half, D, dtype=BF), shape(half, D)]
    return whole(kernel, shapes, "input_grad_sum", (kept, come), deps)


def chunk_pair(right, right_next, deps):
    def kernel(a, b, out):
        out[0:1] = a[...]
        out[1:2] = b[...]

    return whole(kernel, [shape(2, R, TILE, dtype=BF)], "chunk_pair", (right, right_next), deps)[0]


def right_last(kept, come, deps):
    def kernel(kept_ref, come_ref, out):
        out[...] = (kept_ref[...] + come_ref[...].astype(F32)).astype(BF)

    return whole(kernel, [shape(1, R, TILE, dtype=BF)], "right_sum", (kept, come), deps)[0]


def copied_whole(value, deps, flops=1000):
    def kernel(ref, out):
        out[...] = ref[...]

    return whole(kernel, [shape(*value.shape, dtype=value.dtype)], "copied", (value,), deps, flops)[0]


def eliminated(gram):
    rows = lax.broadcasted_iota(jnp.int32, (R, 2 * R), 0)
    lanes = lax.broadcasted_iota(jnp.int32, (R, 2 * R), 1)
    work = jnp.concatenate([gram, jnp.zeros((R, R), F32)], axis=1)
    work = jnp.where(lanes == rows + R, 1.0, work)
    scales = []
    for j in range(0, R, 8):
        columns = [jnp.broadcast_to(work[:, j + k : j + k + 1], (R, 2 * R)) for k in range(8)]
        block = [work[j + k : j + k + 1, :] for k in range(8)]
        for k in range(8):
            pivot = columns[k][j + k : j + k + 1, :]
            inverse = 1.0 / pivot
            scales.append(block[k] * lax.rsqrt(pivot))
            row = block[k] * inverse
            for m in range(k + 1, 8):
                factor = columns[k][j + m : j + m + 1, :]
                columns[m] = columns[m] - columns[k] * (factor * inverse)
                block[m] = block[m] - row * factor
            work = work - jnp.where(rows > j + k, columns[k], 0.0) * row
    return jnp.concatenate(scales, axis=0)[:, R:]


def exact(op, a, b):
    a1, a2, a3 = pieces(a, 3)
    b1, b2, b3 = pieces(b, 3)
    low = op(a1, b3) + op(a2, b2) + op(a3, b1)
    return op(a1, b1) + (op(a1, b2) + op(a2, b1) + low)


def basis_kernel(raw_a, raw_b, unit, z, left, left_t):
    index, _, _, _ = place()
    raw = raw_a[...] + raw_b[...]
    inverse = eliminated(exact(nt, raw, raw))
    parts = jnp.concatenate(pieces(exact(nn, inverse, raw), 3), axis=0)
    z3 = nn(parts, unit[...])
    z[...] = jnp.concatenate(pieces(z3[0:R] + z3[R : 2 * R] + z3[2 * R : 3 * R], 2), axis=0)
    select = selection(index)
    own3 = nt(select, parts)
    left[...] = own3[:, 0:R] + own3[:, R : 2 * R] + own3[:, 2 * R : 3 * R]
    own_t = nt(parts, select)
    left_t[...] = own_t[0:R] + own_t[R : 2 * R] + own_t[2 * R : 3 * R]


def basis_call(raw_a, raw_b, unit, deps):
    return whole(
        basis_kernel,
        [shape(2 * R, F, dtype=BF), shape(32, R), shape(R, 32)],
        "left_factor",
        (raw_a, raw_b, unit),
        deps,

    )


def factor_kernel(z, left_t, weight, resid, feedback, own_out, other_out):
    _, _, x, core = place()
    l1, l2 = pieces(left_t[...], 2)
    for step in range(STEPS):
        columns = slice(step * TILE, (step + 1) * TILE)
        both = nt(z[...], weight[columns, :])
        value = both[0:R] + both[R : 2 * R]
        r1, r2 = pieces(resid[:, columns].astype(F32) + feedback[:, columns], 2)
        value = value + (nn(l1, r1) + (nn(l1, r2) + nn(l2, r1)))
        c = step // 4
        apart = xor_x(step % 4, x)
        spot = jnp.where(apart == 0, 3, jnp.where(apart == 2, 0, jnp.where(apart == 1 + 2 * c, 1, 2)))

        @pl.when(core == c)
        def _():
            own_out[spot] = value

        @pl.when(core != c)
        def _():
            other_out[spot] = value.astype(BF)


def factor_call(z, left_t, weight, resid, feedback, deps):
    return whole(
        factor_kernel,
        [shape(4, R, TILE), shape(4, R, TILE, dtype=BF)],
        "right_factor",
        (z, left_t, weight, resid, feedback),
        deps,
    )


def right_step(total, come, deps):
    keep = total.shape[0] // 2

    def kernel(total_ref, come_ref, send, kept):
        value = total_ref[...] + come_ref[...].astype(F32)
        send[...] = value[0:keep].astype(BF)
        kept[...] = value[keep:]

    shapes = [shape(keep, R, TILE, dtype=BF), shape(keep, R, TILE)]
    return whole(kernel, shapes, "right_sum", (total, come), deps)


def right_sum(total, come, deps):
    def kernel(total_ref, come_ref, send, kept):
        value = total_ref[...] + come_ref[...].astype(F32)
        send[...] = value.astype(BF)
        kept[...] = value

    shapes = [shape(*total.shape, dtype=BF), shape(*total.shape)]
    return whole(kernel, shapes, "right_sum", (total, come), deps)


def grad_call(tokens, ordered, quarter, earlier, deps):
    count = len(earlier) + len(deps)
    ins = len(tokens)

    def kernel(*refs):
        unit, out, token, held, sems = refs[ins], *refs[ins + 1 + count :]
        copies = []
        for k in (0, 1):
            start = (quarter * 2 + k) * TILE
            columns = slice(start, start + TILE)
            blocks = []
            for near, far in (refs[0:2], refs[2:4]):
                for group in (3, 1, 2, 0):
                    rows = slice(group * 32, group * 32 + 32)
                    blocks += [far[rows, columns], near[rows, columns]]
            held[k] = tn(jnp.concatenate(blocks, axis=0), unit[...]).astype(BF)
            copies.append(pltpu.make_async_copy(held.at[k], out.at[pl.ds(start, TILE)], sems.at[k]))
            copies[-1].start()
        token[...] = jnp.zeros((8, 128), F32)
        for copy in copies:
            copy.wait()

    return pl.pallas_call(
        kernel,
        in_specs=[VMEM] * (ins + 1) + [ANY] * count,
        out_specs=[ANY, VMEM],
        out_shape=[shape(D, F, dtype=BF), TOKEN],
        scratch_shapes=[pltpu.VMEM((2, TILE, F), BF), pltpu.SemaphoreType.DMA((2,))],
        input_output_aliases={ins + 1: 0} if earlier else {},
        compiler_params=params(),
        cost_estimate=pl.CostEstimate(flops=1000, bytes_accessed=1000, transcendentals=0),
        name="weight_grad_part",
    )(*tokens, ordered, *earlier, *deps)


def final_kernel(*refs):
    chunks, (left, left_next, resid, feedback, mine, partner, out, received) = refs[:8], refs[8:]
    _, _, x, core = place()
    l3 = jnp.concatenate(pieces(left[...], 2), axis=0)
    n3 = jnp.concatenate(pieces(left_next[...], 2), axis=0)
    for h in (0, 1):
        c = core if h == 0 else 1 - core
        first, second = 1 + 2 * c, 3 - 2 * c
        for k, xx in enumerate((xor_x(x, 2), xor_x(x, first), xor_x(x, second), x)):
            columns = pl.ds(pl.multiple_of((c * 4 + xx) * TILE, 128), TILE)
            chunk = chunks[h * 4 + k]
            here = nn(l3, chunk[0])
            there = nn(n3, chunk[1])
            merged = resid[:, columns].astype(F32) + feedback[:, columns]
            merged = merged + (mine[:, columns] + partner[:, columns].astype(F32))
            out[:, columns] = merged - (here[0:32] + here[32:64])
            received[:, columns] = there[0:32] + there[32:64]


def final_call(chunks, left, left_next, resid, feedback, mine, partner):
    vmem = pl.BlockSpec(memory_space=pltpu.VMEM)
    return pl.pallas_call(
        final_kernel,
        in_specs=[vmem] * 14,
        out_specs=[vmem, vmem],
        out_shape=[jax.ShapeDtypeStruct((32, D), F32)] * 2,
        compiler_params=params(),
        cost_estimate=pl.CostEstimate(flops=1000, bytes_accessed=1000, transcendentals=0),
        name="feedback_and_received",
    )(*chunks, left, left_next, resid, feedback, mine, partner)


def sent(value, move):
    pairs = []
    for index in range(16):
        y, x, core = move(index // 8, (index // 2) % 4, index % 2)
        pairs.append((index, y * 8 + x * 2 + core))
    return lax.ppermute(value, "fsdp", pairs)


def to_core(value):
    return sent(value, lambda y, x, c: (y, x, 1 - c))


def to_first(value):
    return sent(value, lambda y, x, c: (y, x ^ (1 + 2 * c), c))


def to_second(value):
    return sent(value, lambda y, x, c: (y, x ^ (3 - 2 * c), c))


def to_far(value):
    return sent(value, lambda y, x, c: (y, x ^ 2, c))


def to_y(value):
    return sent(value, lambda y, x, c: (1 - y, x, c))


def to_previous(value):
    return lax.ppermute(value, "section", [(s, s - 1) for s in range(1, 8)])


def on_device(activations, gate_preact, hidden_grad, up_weight, resid_grad, feedback, start_basis):
    acts, resid, fb = activations[0], resid_grad[0], feedback[0]
    basis_t = jnp.swapaxes(start_basis[0], 0, 1)

    weight = up_weight[0]
    first_acts = copied_whole(acts, (), 20_000_000_000)
    moved_first, moved_second, acts_y = to_first(first_acts), to_second(first_acts), to_y(first_acts)
    unit, ordered, raw = unit_call(gate_preact[0], hidden_grad[0], weight, basis_t, resid, fb, ())

    come = to_core(raw)
    *parts, token = partial_call(ordered, weight, 0, (), (raw,))
    raw = added(raw, come, (token, moved_first, moved_second))
    late = (raw,)
    gone_first = to_first(stacked((acts_y,), late))
    gone_second = to_second(stacked((acts_y, moved_first), late))
    come = to_y(raw)
    *parts, token = partial_call(ordered, weight, 1, parts, (raw,))
    raw = added(raw, come, (token,))
    come = to_first(raw)
    *parts, token = partial_call(ordered, weight, 2, parts, (raw,))
    other, own, token = partial_call(ordered, weight, 3, parts, (token,))
    raw = added(raw, come, (token, gone_first, gone_second))
    gone_far = to_first(gone_second[0:32])
    near = stacked((acts, moved_first, moved_second, gone_second[32:64]), (raw,))
    come = to_second(raw)
    come_grad = to_core(stacked((other,), (raw,)))

    far = stacked((acts_y, gone_first, gone_second[0:32], gone_far), (come,))
    send, grad_kept = grad_start(own, come_grad, (come, far))
    grad_first = to_first(send)
    z, left, left_t = basis_call(raw, come, unit, (send,))
    left_next = to_previous(left)
    own, other = factor_call(z, left_t, weight, resid, fb, ())

    come = to_core(other)
    send, kept = right_step(own, come, ())
    come = to_first(send)
    tokens = [to_core(near), to_core(far), near, far]
    grad, token = grad_call(tokens, ordered, 0, (), (kept,))
    send, kept = right_sum(kept, come, (left_next, token))
    come = to_y(send)
    send, grad_kept = grad_step(grad_kept, grad_first, (kept,))
    grad_second = to_second(send)
    grad, token = grad_call(tokens, ordered, 1, (grad,), (send,))
    grad, token = grad_call(tokens, ordered, 2, (grad,), (token,))
    send, kept = right_step(kept, come, (token,))
    come = to_second(send)
    weight_grad, token = grad_call(tokens, ordered, 3, (grad,), (kept,))
    right = right_last(kept, come, (token,))
    right_next = to_previous(right)
    send, mine = grad_step(grad_kept, grad_second, (right,))
    partner = to_y(send)
    both = chunk_pair(right, right_next, (send,))
    own_chunks = [to_far(both), to_first(both), to_second(both), both]
    chunks = own_chunks + [to_core(value) for value in own_chunks]

    new_feedback, received = final_call(chunks, left, left_next, resid, fb, mine, partner)
    return (weight_grad[None], new_feedback[None], received[None])


def solution(mesh):
    return jax.shard_map(
        on_device,
        mesh=mesh,
        in_specs=(
            P("section", "fsdp", None),
            P("section", None, "fsdp"),
            P("section", None, "fsdp"),
            P("section", None, "fsdp"),
            P("section", "fsdp", None),
            P("section", "fsdp", None),
            P("section", None, None),
        ),
        out_specs=(
            P("section", None, "fsdp"),
            P("section", "fsdp", None),
            P("section", "fsdp", None),
        ),
        check_vma=False,
    )
```

```python
import jax
import jax.numpy as jnp
from jax import lax
from jax.experimental import pallas as pl
from jax.experimental.pallas import tpu as pltpu
from jax.sharding import PartitionSpec as P

D = 5120
F = 896
R = 64
T = 512
TILE = 640
STEPS = D // TILE
BF = jnp.bfloat16
F32 = jnp.float32
VMEM_LIMIT = 24 * 1024 * 1024


def params(limit=VMEM_LIMIT):
    return pltpu.CompilerParams(vmem_limit_bytes=limit)


def place():
    index = lax.axis_index("fsdp")
    y, x, core = index // 8, (index // 2) % 4, index % 2
    return index, y, x, core


def xor_x(x, mask):
    return x + mask - 2 * (x & mask)


def pieces(value, count):
    out = []
    for _ in range(count):
        part = value.astype(BF)
        out.append(part)
        value = value - part.astype(F32)
    return out


def nn(a, b):
    return lax.dot_general(a, b, (((1,), (0,)), ((), ())), preferred_element_type=F32)


def nt(a, b):
    return lax.dot_general(a, b, (((1,), (1,)), ((), ())), preferred_element_type=F32)


def tn(a, b):
    return lax.dot_general(a, b, (((0,), (0,)), ((), ())), preferred_element_type=F32)


def row_blocks(y, x, core):
    out = []
    for c in (1 - core, core):
        first, second = 1 + 2 * c, 3 - 2 * c
        for xx in (xor_x(x, 2), xor_x(x, first), xor_x(x, second), x):
            for yy in (1 - y, y):
                out.append(yy * 8 + xx * 2 + c)
    return out


def unit_kernel(gate, hidden, weight, basis_t, resid, feedback, unit, ordered, raw_t):
    index, y, x, core = place()
    wb = jnp.zeros((3 * R, F), F32)
    own = jnp.zeros((R, 32), F32)
    for i in range(STEPS):
        columns = slice(i * TILE, (i + 1) * TILE)
        split = jnp.concatenate(pieces(basis_t[:, columns], 3), axis=0)
        rows = jnp.concatenate(pieces(resid[:, columns].astype(F32) + feedback[:, columns], 3), axis=0)
        rb = nt(split, rows)
        rb = rb[0:R] + rb[R : 2 * R] + rb[2 * R : 3 * R]
        own = own + (rb[:, 0:32] + rb[:, 32:64] + rb[:, 64:96])
        wb = wb + nn(split, weight[columns, :])
        for k in range(2 * i, 2 * i + 2):
            rows = slice(k * 32, (k + 1) * 32)
            g = gate[rows].astype(F32)
            unit[rows] = (hidden[rows].astype(F32) * (g / (1.0 + jnp.exp(-g)))).astype(BF)
    for place_to, block in enumerate(row_blocks(y, x, core)):
        ordered[pl.ds(place_to * 32, 32), :] = unit[pl.ds(pl.multiple_of(block * 32, 32), 32), :]
    total = wb[0:R, :] + wb[R : 2 * R, :] + wb[2 * R : 3 * R, :]
    raw3 = nt(jnp.concatenate(pieces(total, 3), axis=0), unit[...])
    raw = raw3[0:R] + raw3[R : 2 * R] + raw3[2 * R : 3 * R]
    placed = nn(jnp.concatenate(pieces(own, 3), axis=0), selection(index))
    raw_t[...] = raw + placed[0:R] + placed[R : 2 * R] + placed[2 * R : 3 * R]


def selection(index):
    spot = lax.broadcasted_iota(jnp.int32, (32, T), 1) - index * 32
    return (spot == lax.broadcasted_iota(jnp.int32, (32, T), 0)).astype(BF)


VMEM = pl.BlockSpec(memory_space=pltpu.VMEM)
ANY = pl.BlockSpec(memory_space=pl.ANY)
TOKEN = jax.ShapeDtypeStruct((8, 128), F32)


def whole(kernel, out_shape, name, operands, deps=(), flops=1000, out_specs=None, scratch=(), in_specs=None, limit=VMEM_LIMIT):
    count = len(operands)

    def body(*refs):
        kernel(*refs[:count], *refs[count + len(deps) :])

    return pl.pallas_call(
        body,
        in_specs=(in_specs or [VMEM] * count) + [ANY] * len(deps),
        out_specs=out_specs or [VMEM] * len(out_shape),
        out_shape=out_shape,
        scratch_shapes=list(scratch),
        compiler_params=params(limit),
        cost_estimate=pl.CostEstimate(flops=flops, bytes_accessed=1000, transcendentals=0),
        name=name,
    )(*operands, *deps)


def shape(*dims, dtype=F32):
    return jax.ShapeDtypeStruct(dims, dtype)


def unit_call(gate, hidden, weight, basis_t, resid, feedback, deps):
    return whole(
        unit_kernel,
        [shape(T, F, dtype=BF), shape(T, F, dtype=BF), shape(R, T)],
        "unit_and_raw",
        (gate, hidden, weight, basis_t, resid, feedback),
        deps,
        flops=20_000_000_000,
    )


def partial_call(ordered, weight, quarter, earlier, deps):
    column = lambda i: (0, quarter * 2 + i)
    count = len(earlier) + len(deps)

    def kernel(unit, held, *refs):
        rows = pl.ds(pl.multiple_of((quarter * 2 + pl.program_id(0)) * TILE, TILE), TILE)
        product = nt(unit[...], held[rows, :])
        refs[count][...] = product[0:256].astype(BF)
        refs[count + 1][...] = product[256:512]
        refs[-1][...] = jnp.zeros((8, 128), F32)

    return pl.pallas_call(
        kernel,
        grid=(2,),
        in_specs=[VMEM, VMEM] + [ANY] * count,
        out_specs=[pl.BlockSpec((256, TILE), column)] * 2 + [pl.BlockSpec((8, 128), lambda i: (0, 0))],
        out_shape=[shape(256, D, dtype=BF), shape(256, D), TOKEN],
        input_output_aliases={2 + k: k for k in range(len(earlier))},
        compiler_params=params(),
        cost_estimate=pl.CostEstimate(flops=1000, bytes_accessed=1000, transcendentals=0),
        name="input_grad_part",
    )(ordered, weight, *earlier, *deps)


def added(a, b, deps=()):
    def kernel(a_ref, b_ref, out):
        out[...] = a_ref[...] + b_ref[...]

    return whole(kernel, [shape(*a.shape)], "raw_sum", (a, b), deps)[0]


def stacked(values, deps):
    rows = values[0].shape[0]

    def kernel(*refs):
        for k, ref in enumerate(refs[:-1]):
            refs[-1][k * rows : (k + 1) * rows] = ref[...]

    return whole(kernel, [shape(len(values) * rows, D, dtype=BF)], "stack", values, deps)[0]


def grad_start(own, come, deps):
    def kernel(own_ref, come_ref, send, kept):
        send[...] = (own_ref[0:128] + come_ref[0:128].astype(F32)).astype(BF)
        kept[...] = own_ref[128:256] + come_ref[128:256].astype(F32)

    shapes = [shape(128, D, dtype=BF), shape(128, D)]
    return whole(kernel, shapes, "input_grad_sum", (own, come), deps)


def grad_step(kept, come, deps):
    half = kept.shape[0] // 2

    def kernel(kept_ref, come_ref, send, out):
        send[...] = (kept_ref[0:half] + come_ref[0:half].astype(F32)).astype(BF)
        out[...] = kept_ref[half:] + come_ref[half:].astype(F32)

    shapes = [shape(half, D, dtype=BF), shape(half, D)]
    return whole(kernel, shapes, "input_grad_sum", (kept, come), deps)


def chunk_pair(right, right_next, deps):
    def kernel(a, b, out):
        out[0:1] = a[...]
        out[1:2] = b[...]

    return whole(kernel, [shape(2, R, TILE, dtype=BF)], "chunk_pair", (right, right_next), deps)[0]


def right_last(kept, come, deps):
    def kernel(kept_ref, come_ref, out):
        out[...] = (kept_ref[...] + come_ref[...].astype(F32)).astype(BF)

    return whole(kernel, [shape(1, R, TILE, dtype=BF)], "right_sum", (kept, come), deps)[0]


def copied_whole(value, deps, flops=1000):
    def kernel(ref, out):
        out[...] = ref[...]

    return whole(kernel, [shape(*value.shape, dtype=value.dtype)], "copied", (value,), deps, flops)[0]


def eliminated(gram):
    rows = lax.broadcasted_iota(jnp.int32, (R, 2 * R), 0)
    lanes = lax.broadcasted_iota(jnp.int32, (R, 2 * R), 1)
    work = jnp.concatenate([gram, jnp.zeros((R, R), F32)], axis=1)
    work = jnp.where(lanes == rows + R, 1.0, work)
    scales = []
    for j in range(0, R, 8):
        columns = [jnp.broadcast_to(work[:, j + k : j + k + 1], (R, 2 * R)) for k in range(8)]
        block = [work[j + k : j + k + 1, :] for k in range(8)]
        for k in range(8):
            pivot = columns[k][j + k : j + k + 1, :]
            inverse = 1.0 / pivot
            scales.append(block[k] * lax.rsqrt(pivot))
            row = block[k] * inverse
            for m in range(k + 1, 8):
                factor = columns[k][j + m : j + m + 1, :]
                columns[m] = columns[m] - columns[k] * (factor * inverse)
                block[m] = block[m] - row * factor
            work = work - jnp.where(rows > j + k, columns[k], 0.0) * row
    return jnp.concatenate(scales, axis=0)[:, R:]


def exact(op, a, b):
    a1, a2, a3 = pieces(a, 3)
    b1, b2, b3 = pieces(b, 3)
    low = op(a1, b3) + op(a2, b2) + op(a3, b1)
    return op(a1, b1) + (op(a1, b2) + op(a2, b1) + low)


def basis_kernel(raw_a, raw_b, unit, z, left, left_t):
    index, _, _, _ = place()
    raw = raw_a[...] + raw_b[...]
    inverse = eliminated(exact(nt, raw, raw))
    parts = jnp.concatenate(pieces(exact(nn, inverse, raw), 3), axis=0)
    z3 = nn(parts, unit[...])
    z[...] = jnp.concatenate(pieces(z3[0:R] + z3[R : 2 * R] + z3[2 * R : 3 * R], 2), axis=0)
    select = selection(index)
    own3 = nt(select, parts)
    left[...] = own3[:, 0:R] + own3[:, R : 2 * R] + own3[:, 2 * R : 3 * R]
    own_t = nt(parts, select)
    left_t[...] = own_t[0:R] + own_t[R : 2 * R] + own_t[2 * R : 3 * R]


def basis_call(raw_a, raw_b, unit, deps):
    return whole(
        basis_kernel,
        [shape(2 * R, F, dtype=BF), shape(32, R), shape(R, 32)],
        "left_factor",
        (raw_a, raw_b, unit),
        deps,

    )


def factor_kernel(z, left, weight, resid, feedback, own_out, other_out):
    _, _, x, core = place()
    l1, l2 = pieces(left[...], 2)
    own_left = jnp.concatenate([l1, l1, l2], axis=0)
    for step in range(STEPS):
        columns = slice(step * TILE, (step + 1) * TILE)
        both = nt(z[...], weight[columns, :])
        value = both[0:R] + both[R : 2 * R]
        r1, r2 = pieces(resid[:, columns].astype(F32) + feedback[:, columns], 2)
        value = value + tn(own_left, jnp.concatenate([r1, r2, r1], axis=0))
        c = step // 4
        apart = xor_x(step % 4, x)
        spot = jnp.where(apart == 0, 3, jnp.where(apart == 2, 0, jnp.where(apart == 1 + 2 * c, 1, 2)))

        @pl.when(core == c)
        def _():
            own_out[spot] = value

        @pl.when(core != c)
        def _():
            other_out[spot] = value.astype(BF)


def factor_call(z, left, weight, resid, feedback, deps):
    return whole(
        factor_kernel,
        [shape(4, R, TILE), shape(4, R, TILE, dtype=BF)],
        "right_factor",
        (z, left, weight, resid, feedback),
        deps,
    )


def right_step(total, come, deps):
    keep = total.shape[0] // 2

    def kernel(total_ref, come_ref, send, kept):
        value = total_ref[...] + come_ref[...].astype(F32)
        send[...] = value[0:keep].astype(BF)
        kept[...] = value[keep:]

    shapes = [shape(keep, R, TILE, dtype=BF), shape(keep, R, TILE)]
    return whole(kernel, shapes, "right_sum", (total, come), deps)


def right_sum(total, come, deps):
    def kernel(total_ref, come_ref, send, kept):
        value = total_ref[...] + come_ref[...].astype(F32)
        send[...] = value.astype(BF)
        kept[...] = value

    shapes = [shape(*total.shape, dtype=BF), shape(*total.shape)]
    return whole(kernel, shapes, "right_sum", (total, come), deps)


def grad_call(tokens, ordered, quarter, earlier, deps):
    count = len(earlier) + len(deps)
    ins = len(tokens)

    def kernel(*refs):
        unit, out, token, held, sems = refs[ins], *refs[ins + 1 + count :]
        copies = []
        for k in (0, 1):
            start = (quarter * 2 + k) * TILE
            columns = slice(start, start + TILE)
            blocks = []
            for near, far in (refs[0:2], refs[2:4]):
                for group in (3, 1, 2, 0):
                    rows = slice(group * 32, group * 32 + 32)
                    blocks += [far[rows, columns], near[rows, columns]]
            held[k] = tn(jnp.concatenate(blocks, axis=0), unit[...]).astype(BF)
            copies.append(pltpu.make_async_copy(held.at[k], out.at[pl.ds(start, TILE)], sems.at[k]))
            copies[-1].start()
        token[...] = jnp.zeros((8, 128), F32)
        for copy in copies:
            copy.wait()

    return pl.pallas_call(
        kernel,
        in_specs=[VMEM] * (ins + 1) + [ANY] * count,
        out_specs=[ANY, VMEM],
        out_shape=[shape(D, F, dtype=BF), TOKEN],
        scratch_shapes=[pltpu.VMEM((2, TILE, F), BF), pltpu.SemaphoreType.DMA((2,))],
        input_output_aliases={ins + 1: 0} if earlier else {},
        compiler_params=params(),
        cost_estimate=pl.CostEstimate(flops=1000, bytes_accessed=1000, transcendentals=0),
        name="weight_grad_part",
    )(*tokens, ordered, *earlier, *deps)


def final_kernel(*refs):
    chunks, (left, left_next, resid, feedback, mine, partner, out, received) = refs[:8], refs[8:]
    _, _, x, core = place()
    l3 = jnp.concatenate(pieces(left[...], 2), axis=0)
    n3 = jnp.concatenate(pieces(left_next[...], 2), axis=0)
    for h in (0, 1):
        c = core if h == 0 else 1 - core
        first, second = 1 + 2 * c, 3 - 2 * c
        for k, xx in enumerate((xor_x(x, 2), xor_x(x, first), xor_x(x, second), x)):
            columns = pl.ds(pl.multiple_of((c * 4 + xx) * TILE, 128), TILE)
            chunk = chunks[h * 4 + k]
            here = nn(l3, chunk[0])
            there = nn(n3, chunk[1])
            merged = resid[:, columns].astype(F32) + feedback[:, columns]
            merged = merged + (mine[:, columns] + partner[:, columns].astype(F32))
            out[:, columns] = merged - (here[0:32] + here[32:64])
            received[:, columns] = there[0:32] + there[32:64]


def final_call(chunks, left, left_next, resid, feedback, mine, partner):
    vmem = pl.BlockSpec(memory_space=pltpu.VMEM)
    return pl.pallas_call(
        final_kernel,
        in_specs=[vmem] * 14,
        out_specs=[vmem, vmem],
        out_shape=[jax.ShapeDtypeStruct((32, D), F32)] * 2,
        compiler_params=params(),
        cost_estimate=pl.CostEstimate(flops=1000, bytes_accessed=1000, transcendentals=0),
        name="feedback_and_received",
    )(*chunks, left, left_next, resid, feedback, mine, partner)


def sent(value, move):
    pairs = []
    for index in range(16):
        y, x, core = move(index // 8, (index // 2) % 4, index % 2)
        pairs.append((index, y * 8 + x * 2 + core))
    return lax.ppermute(value, "fsdp", pairs)


def to_core(value):
    return sent(value, lambda y, x, c: (y, x, 1 - c))


def to_first(value):
    return sent(value, lambda y, x, c: (y, x ^ (1 + 2 * c), c))


def to_second(value):
    return sent(value, lambda y, x, c: (y, x ^ (3 - 2 * c), c))


def to_far(value):
    return sent(value, lambda y, x, c: (y, x ^ 2, c))


def to_y(value):
    return sent(value, lambda y, x, c: (1 - y, x, c))


def to_previous(value):
    return lax.ppermute(value, "section", [(s, s - 1) for s in range(1, 8)])


def on_device(activations, gate_preact, hidden_grad, up_weight, resid_grad, feedback, start_basis):
    acts, resid, fb = activations[0], resid_grad[0], feedback[0]
    basis_t = jnp.swapaxes(start_basis[0], 0, 1)

    weight = up_weight[0]
    first_acts = copied_whole(acts, (), 20_000_000_000)
    moved_first, moved_second, acts_y = to_first(first_acts), to_second(first_acts), to_y(first_acts)
    unit, ordered, raw = unit_call(gate_preact[0], hidden_grad[0], weight, basis_t, resid, fb, ())

    come = to_core(raw)
    *parts, token = partial_call(ordered, weight, 0, (), (raw,))
    raw = added(raw, come, (token, moved_first, moved_second))
    late = (raw,)
    gone_first = to_first(stacked((acts_y,), late))
    gone_second = to_second(stacked((acts_y, moved_first), late))
    come = to_y(raw)
    *parts, token = partial_call(ordered, weight, 1, parts, (raw,))
    raw = added(raw, come, (token,))
    come = to_first(raw)
    *parts, token = partial_call(ordered, weight, 2, parts, (raw,))
    other, own, token = partial_call(ordered, weight, 3, parts, (token,))
    raw = added(raw, come, (token, gone_first, gone_second))
    gone_far = to_first(gone_second[0:32])
    near = stacked((acts, moved_first, moved_second, gone_second[32:64]), (raw,))
    come = to_second(raw)
    come_grad = to_core(stacked((other,), (raw,)))

    far = stacked((acts_y, gone_first, gone_second[0:32], gone_far), (come,))
    send, grad_kept = grad_start(own, come_grad, (come, far))
    grad_first = to_first(send)
    z, left, left_t = basis_call(raw, come, unit, (send,))
    left_next = to_previous(left)
    own, other = factor_call(z, left, weight, resid, fb, ())

    come = to_core(other)
    send, kept = right_step(own, come, ())
    come = to_first(send)
    tokens = [to_core(near), to_core(far), near, far]
    grad, token = grad_call(tokens, ordered, 0, (), (kept,))
    send, kept = right_sum(kept, come, (left_next, token))
    come = to_y(send)
    send, grad_kept = grad_step(grad_kept, grad_first, (kept,))
    grad_second = to_second(send)
    grad, token = grad_call(tokens, ordered, 1, (grad,), (send,))
    grad, token = grad_call(tokens, ordered, 2, (grad,), (token,))
    send, kept = right_step(kept, come, (token,))
    come = to_second(send)
    weight_grad, token = grad_call(tokens, ordered, 3, (grad,), (kept,))
    right = right_last(kept, come, (token,))
    right_next = to_previous(right)
    send, mine = grad_step(grad_kept, grad_second, (right,))
    partner = to_y(send)
    both = chunk_pair(right, right_next, (send,))
    own_chunks = [to_far(both), to_first(both), to_second(both), both]
    chunks = own_chunks + [to_core(value) for value in own_chunks]

    new_feedback, received = final_call(chunks, left, left_next, resid, fb, mine, partner)
    return (weight_grad[None], new_feedback[None], received[None])


def solution(mesh):
    return jax.shard_map(
        on_device,
        mesh=mesh,
        in_specs=(
            P("section", "fsdp", None),
            P("section", None, "fsdp"),
            P("section", None, "fsdp"),
            P("section", None, "fsdp"),
            P("section", "fsdp", None),
            P("section", "fsdp", None),
            P("section", None, None),
        ),
        out_specs=(
            P("section", None, "fsdp"),
            P("section", "fsdp", None),
            P("section", "fsdp", None),
        ),
        check_vma=False,
    )
```
